32 devices in a mesh: ctx: 8 (over z, x), tp: 2 (over core), ep: 2 (over y).
Axes of the slice: x: 2, y: 2, z: 4, core: 2. Of those that a mesh axis runs over, the one named last changes fastest.
Arguments:
- hidden: bfloat16 [1024, 3584], P('ctx'), may hold values from -40 to 40
- grad_out: bfloat16 [1024, 3584], P('ctx'), may hold values from -6 to 6
- gain: float32 [3584], replicated, may hold values from 0.5 to 1.5
- dense_gate: bfloat16 [2432, 3584], P(('tp', 'ep')), may hold values from -0.09375 to 0.09375
- dense_up: bfloat16 [2432, 3584], P(('tp', 'ep')), may hold values from -0.09375 to 0.09375
- dense_down: bfloat16 [2432, 3584], P(('tp', 'ep')), may hold values from -0.125 to 0.125
- expert_gate: bfloat16 [8, 3840, 3584], P('ctx', ('tp', 'ep')), may hold values from -0.09375 to 0.09375
- expert_up: bfloat16 [8, 3840, 3584], P('ctx', ('tp', 'ep')), may hold values from -0.09375 to 0.09375
- expert_down: bfloat16 [8, 3840, 3584], P('ctx', ('tp', 'ep')), may hold values from -0.09375 to 0.09375
- out_proj: bfloat16 [1024, 3584], P(('tp', 'ep')), may hold values from -0.1875 to 0.1875
- queries: bfloat16 [1024, 1024], P('ctx', ('tp', 'ep')), may hold values from -12 to 12
- keys: bfloat16 [1024, 1024], P('ctx', ('tp', 'ep')), may hold values from -12 to 12
- values: bfloat16 [1024, 1024], P('ctx', ('tp', 'ep')), may hold values from -6 to 6
- route_ids: int32 [1024, 2], P('ctx'), may hold values from 0 to 7, all different within a row; in each aligned block of 128 rows (0 to 127, 128 to 255, ...) at most 40 rows name the same one
- route_weights: float32 [1024, 2], P('ctx'), may hold values from 0.2 to 1
Outputs:
- grad_hidden: bfloat16 [1024, 3584], P('ctx')
- grad_queries: bfloat16 [1024, 1024], P('ctx', ('tp', 'ep'))
- grad_keys: bfloat16 [1024, 1024], P('ctx', ('tp', 'ep'))
- grad_values: bfloat16 [1024, 1024], P('ctx', ('tp', 'ep'))
The draws below stay inside these ranges and needn't reach their ends.
Inputs may be any that keep to these rules, and one draw needn't show every extreme that they name: `route_ids`: the two ids of a token differ. In each aligned block of 128 tokens no expert is named by more than 40 routed rows, a bound that some block reaches.
All inputs are finite; a program needn't handle non-finite values.
Results may differ from the reference program's by a relative error of at most 0.03.
Values may be sent and summed in bfloat16 or wider, within the bound.
A program may use at most 128 MiB of HBM per device.

```python
import math
import jax
import jax.numpy as jnp
import numpy as np
from jax import lax

D = 3584
HEAD_DIM = 128
FF = 2432
EH = 3840
BLOCK = 128
SEQ = 1024
HEADS = 8
EXPERTS = 8
CAP = 40
N_CTX = 8


def draw_queries(key, part):
    key = jax.random.fold_in(key, 11)
    base = jnp.clip(jax.random.normal(key, (SEQ, HEADS * HEAD_DIM), jnp.float32), -4.0, 4.0)
    return base.astype(jnp.bfloat16)


def draw_keys(key, part):
    key = jax.random.fold_in(key, 12)
    base = jnp.clip(jax.random.normal(key, (SEQ, HEADS * HEAD_DIM), jnp.float32), -4.0, 4.0)
    return base.astype(jnp.bfloat16)


def draw_hidden(key, part):
    key = jax.random.fold_in(key, 21)
    base_key, row_key, col_key = jax.random.split(key, 3)
    row_scale = jnp.exp(jax.random.uniform(row_key, (SEQ, 1), jnp.float32, math.log(0.3), math.log(3.0)))
    col_scale = jnp.exp(jax.random.uniform(col_key, (1, D), jnp.float32, math.log(0.3), math.log(3.0)))
    base = jnp.clip(jax.random.normal(base_key, (SEQ, D), jnp.float32), -4.0, 4.0)
    return (base * row_scale * col_scale).astype(jnp.bfloat16)


def level_of(own_key, dims, cuts, low, top_value):
    loudness = 1.0
    for axis_at, parts in cuts:
        heights = jax.random.uniform(jax.random.fold_in(jax.random.fold_in(own_key, 6), axis_at), (parts,), jnp.float32, low / len(cuts), top_value / len(cuts))
        loudness = loudness * jnp.repeat(jnp.exp(heights), dims[axis_at] // parts).reshape((-1,) + (1,) * (len(dims) - 1 - axis_at))
    return loudness


def assign_block(own_key, own, number, rows, number_of, top, bound, skew):
    ranking = jax.random.permutation(own_key, number_of)
    crowded, ordinary = shares(number_of, rows * top, bound, skew, True), shares(number_of, rows * top, bound, skew, False)
    places = jnp.arange(number_of)

    def named(tallies, offset_by):
        used = int((tallies > 0).sum())
        fixed = max(1, used // 4)
        shifted = fixed + (places - fixed + offset_by * (used - fixed)) % max(1, number_of - fixed)
        return jnp.zeros((number_of,), jnp.int32).at[ranking[jnp.where(places < fixed, places, shifted)]].set(jnp.asarray(tallies, jnp.int32))

    tallies = jnp.where(number % 4 == 0, named(crowded, number // 4), named(ordinary, number - number // 4 - 1))
    mixed = jax.random.permutation(jax.random.fold_in(own, 3), number_of)
    giver, receiver = mixed[0:number_of // 2 * 2:2], mixed[1:number_of // 2 * 2:2]
    room = jnp.minimum(tallies[giver] - 1, bound - tallies[receiver]) // 2
    room = jnp.where((giver == ranking[0]) | (receiver == ranking[0]) | (tallies[receiver] == 0), 0, jnp.maximum(room, 0))
    shifted = jax.random.randint(jax.random.fold_in(own, 4), (number_of // 2,), 0, 1 << 20) % (room + 1)
    tallies = tallies.at[giver].add(-shifted).at[receiver].add(shifted)
    items = jnp.searchsorted(jnp.cumsum(tallies), jnp.arange(rows * top), side="right").astype(jnp.int32)
    table = items.reshape(top, rows).T
    table = table[jax.random.permutation(jax.random.fold_in(own, 1), rows)]
    offset_by = jax.random.randint(jax.random.fold_in(own, 2), (rows, 1), 0, top)
    return jnp.take_along_axis(table, (jnp.arange(top)[None, :] + offset_by) % top, axis=1)


def shares(amount, total, bound, skew, full):
    loads = [(1 << 20) // math.isqrt(rank ** skew) + 1 for rank in range(1, amount + 1)]
    largest = bound if full else min(bound, max(-(-total // amount), total * loads[0] // sum(loads)))
    least = 1 if total - largest >= amount - 1 else 0
    counts, surplus = [largest] + [least] * (amount - 1), total - largest - least * (amount - 1)
    while surplus > 0:
        movable = [i for i in range(1, amount) if counts[i] < largest] or [i for i in range(1, amount) if counts[i] < bound]
        pool, left = sum([loads[i] for i in movable]), surplus
        for i in movable:
            addition = min(bound - counts[i], max(1, left * loads[i] // pool), surplus)
            counts[i] = counts[i] + addition
            surplus = surplus - addition
    return np.array(counts)


def centred(key, extent, deviation, bound, pieces=(), kind=jnp.bfloat16):
    values = deviation * jax.random.normal(key, extent, jnp.float32)
    if pieces:
        values = values * level_of(key, extent, pieces, -0.22, 0.18)
    return jnp.clip(values, -bound, bound).astype(kind)


def setup_inputs(seed: int = 0) -> dict:
    seeds = jax.random.split(jax.random.key(seed), 16)
    hidden = draw_hidden(jax.random.fold_in(seeds[15], 71), 0)
    grad_out = centred(seeds[1], (SEQ, D), 1.0, 6.0, ((0, 8),))
    gain = jnp.clip(1.0 + 0.1 * jax.random.normal(seeds[2], (D,), jnp.float32), 0.5, 1.5)
    dense_gate = centred(seeds[3], (FF, D), D ** -0.5, 0.09375, ((0, 4),))
    dense_up = centred(seeds[4], (FF, D), D ** -0.5, 0.09375, ((0, 4),))
    dense_down = centred(seeds[5], (FF, D), FF ** -0.5, 0.125, ((0, 4),))
    expert_gate = centred(seeds[6], (EXPERTS, EH, D), D ** -0.5, 0.09375, ((0, 8), (1, 4)))
    expert_up = centred(seeds[7], (EXPERTS, EH, D), D ** -0.5, 0.09375, ((0, 8), (1, 4)))
    expert_down = centred(seeds[8], (EXPERTS, EH, D), EH ** -0.5, 0.09375, ((0, 8), (1, 4)))
    out_proj = centred(seeds[9], (HEADS * HEAD_DIM, D), (HEADS * HEAD_DIM) ** -0.5, 0.1875, ((0, 4),))
    queries = draw_queries(jax.random.fold_in(seeds[15], 71), 0)
    keys = draw_keys(jax.random.fold_in(seeds[15], 71), 0)
    values = centred(seeds[12], (SEQ, HEADS * HEAD_DIM), 1.0, 6.0, ((0, 8), (1, 4)))
    route_ids_keys = jax.random.split(jax.random.fold_in(seeds[13], 1), SEQ // BLOCK)
    route_ids_turns = jax.random.permutation(jax.random.fold_in(seeds[13], 3), SEQ // BLOCK)
    route_ids = jax.vmap(lambda own, number: assign_block(jax.random.fold_in(seeds[13], 2), own, number, BLOCK, EXPERTS, 2, CAP, 1))(route_ids_keys, route_ids_turns).reshape((SEQ, 2))
    route_weights = jnp.clip(0.2 + 0.8 * jax.random.uniform(seeds[14], (SEQ, 2), jnp.float32) ** level_of(seeds[14], (SEQ, 2), ((0, 8),), -0.2, 0.2), 0.2, 1.0)
    return dict(hidden=hidden, grad_out=grad_out, gain=gain, dense_gate=dense_gate, dense_up=dense_up, dense_down=dense_down, expert_gate=expert_gate, expert_up=expert_up, expert_down=expert_down, out_proj=out_proj, queries=queries, keys=keys, values=values, route_ids=route_ids, route_weights=route_weights)


NEG_FILL = -1e+30
EPSILON = 1e-05

def contract_last(left_rows, right_rows):
    return lax.dot_general(left_rows, right_rows, (((1,), (1,)), ((), ())), preferred_element_type=jnp.float32)

def swiglu_grad(inputs, upstream, w_gate, w_up, w_down):
    gate_pre = contract_last(inputs, w_gate)
    up_pre = contract_last(inputs, w_up)
    back_grad = contract_last(upstream, w_down)
    sigmoid_gate = jax.nn.sigmoid(gate_pre)
    grad_gate = (back_grad * up_pre * sigmoid_gate * (1.0 + gate_pre * (1.0 - sigmoid_gate))).astype(jnp.bfloat16)
    grad_upper = (back_grad * gate_pre * sigmoid_gate).astype(jnp.bfloat16)
    return jnp.dot(grad_gate, w_gate, preferred_element_type=jnp.float32) + jnp.dot(grad_upper, w_up, preferred_element_type=jnp.float32)

def head_grads(operands):
    query_rows, key_rows, value_rows, upstream = operands
    score_scale = HEAD_DIM ** (-0.5)
    position = lax.iota(jnp.int32, SEQ)
    allowed = position[None, :] <= position[:, None]
    scores = jnp.where(allowed, contract_last(query_rows, key_rows) * score_scale, NEG_FILL)
    top_score = lax.optimization_barrier(jnp.max(scores, axis=1, keepdims=True))
    weights = jnp.where(allowed, jnp.exp(scores - top_score), 0.0)
    weight_sum = lax.optimization_barrier(jnp.sum(weights, axis=1, keepdims=True))
    grad_probs = contract_last(upstream, value_rows)
    delta_row = lax.optimization_barrier(jnp.sum(weights * grad_probs, axis=1, keepdims=True)) / weight_sum
    log_norm = top_score + jnp.log(weight_sum)
    probs = jnp.where(allowed, jnp.exp(scores - log_norm), 0.0)
    grad_scores = probs * (grad_probs - delta_row)
    probs_half = probs.astype(jnp.bfloat16)
    grad_half = grad_scores.astype(jnp.bfloat16)
    grad_query = jnp.dot(grad_half, key_rows, preferred_element_type=jnp.float32) * score_scale
    grad_key = jnp.dot(grad_half.T, query_rows, preferred_element_type=jnp.float32) * score_scale
    grad_value = jnp.dot(probs_half.T, upstream, preferred_element_type=jnp.float32)
    return (grad_query.astype(jnp.bfloat16), grad_key.astype(jnp.bfloat16), grad_value.astype(jnp.bfloat16))

def one_expert(operands):
    return swiglu_grad(operands[0], operands[1], operands[2], operands[3], operands[4])

def per_head(array):
    return array.reshape(SEQ, HEADS, HEAD_DIM).transpose(1, 0, 2)

def merge_heads(array):
    return array.transpose(1, 0, 2).reshape(SEQ, HEADS * HEAD_DIM)

def reference(hidden, grad_out, gain, dense_gate, dense_up, dense_down, expert_gate, expert_up, expert_down, out_proj, queries, keys, values, route_ids, route_weights):
    hidden_f = hidden.astype(jnp.float32)
    inverse = lax.rsqrt(lax.optimization_barrier(jnp.mean(hidden_f * hidden_f, axis=1, keepdims=True)) + EPSILON)
    normed = hidden_f * inverse
    mixed_in = (normed * gain).astype(jnp.bfloat16)
    dense_part = swiglu_grad(mixed_in, grad_out, dense_gate, dense_up, dense_down)
    ids_block = route_ids.reshape(N_CTX, 2 * BLOCK)
    hits = (ids_block[:, :, None] == lax.iota(jnp.int32, EXPERTS)[None, None, :]).astype(jnp.int32)
    earlier = jnp.cumsum(hits, axis=1) - hits
    slots = lax.optimization_barrier(jnp.sum(earlier * hits, axis=2))
    places = ids_block * CAP + slots
    owners = lax.iota(jnp.int32, 2 * BLOCK) // 2

    def tables(place_row, weight_row):
        token_of = jnp.full((EXPERTS * CAP,), BLOCK, jnp.int32).at[place_row].set(owners)
        weight_of = jnp.zeros((EXPERTS * CAP,), jnp.float32).at[place_row].set(weight_row)
        return (token_of, weight_of)
    token_of, weight_of = jax.vmap(tables)(places, route_weights.reshape(N_CTX, 2 * BLOCK))
    present = token_of < BLOCK
    picked = jnp.minimum(token_of, BLOCK - 1) + (lax.iota(jnp.int32, N_CTX) * BLOCK)[:, None]
    send_in = jnp.where(present[:, :, None], mixed_in[picked], jnp.zeros((), jnp.bfloat16))
    send_grad = (grad_out[picked].astype(jnp.float32) * weight_of[:, :, None]).astype(jnp.bfloat16)
    expert_in = send_in.reshape(N_CTX, EXPERTS, CAP, D).transpose(1, 0, 2, 3).reshape(EXPERTS, N_CTX * CAP, D)
    expert_back = send_grad.reshape(N_CTX, EXPERTS, CAP, D).transpose(1, 0, 2, 3).reshape(EXPERTS, N_CTX * CAP, D)
    expert_rows = lax.map(one_expert, (expert_in, expert_back, expert_gate, expert_up, expert_down))
    expert_rows = expert_rows.reshape(EXPERTS, N_CTX, CAP, D).transpose(1, 0, 2, 3).reshape(N_CTX, EXPERTS * CAP, D)
    routed = jnp.take_along_axis(expert_rows, places[:, :, None], axis=1).reshape(SEQ, 2, D).sum(axis=1)
    total_grad = dense_part + routed
    scaled_grad = total_grad * gain
    grad_hidden = (grad_out.astype(jnp.float32) + inverse * (scaled_grad - normed * lax.optimization_barrier(jnp.mean(scaled_grad * normed, axis=1, keepdims=True)))).astype(jnp.bfloat16)
    grad_heads = contract_last(grad_hidden, out_proj).astype(jnp.bfloat16)
    grad_queries, grad_keys, grad_values = lax.map(head_grads, (per_head(queries), per_head(keys), per_head(values), per_head(grad_heads)))
    return (grad_hidden, merge_heads(grad_queries), merge_heads(grad_keys), merge_heads(grad_values))
```

```python
import functools

import jax
import jax.numpy as jnp
from jax import lax
from jax.experimental import pallas as pl
from jax.experimental.pallas import tpu as pltpu
from jax.sharding import PartitionSpec as P

HEAD_DIM = 128
NEG_FILL = -1e30
EPSILON = 1e-05
MESH = pl.DeviceIdType.MESH
ANY = pl.BlockSpec(memory_space=pl.ANY)
WHOLE = pl.BlockSpec(memory_space=pltpu.VMEM)
BF16 = jnp.bfloat16
F32 = jnp.float32


def contract_last(left_rows, right_rows):
    return lax.dot_general(
        left_rows, right_rows, (((1,), (1,)), ((), ())), preferred_element_type=F32
    )


def round_up(value, step):
    return -(-value // step) * step


def tile_of(hidden, most):
    fits = [t for t in range(16, most + 1, 16) if hidden % t == 0]
    return max(fits) if fits else hidden


class Place:
    def __init__(self, n, tp, ep):
        self.n, self.tp, self.ep = n, tp, ep
        self.c = lax.axis_index("ctx")
        self.t = lax.axis_index("tp")
        self.e = lax.axis_index("ep")

    def ctx_peer(self, k):
        return lax.rem(self.c + k, self.n)

    def ctx_from(self, k):
        return lax.rem(self.c + self.n - k, self.n)

    def ep_peer(self, b):
        return lax.rem(self.e + b, self.ep)

    def ep_from(self, b):
        return lax.rem(self.e + self.ep - b, self.ep)

    def at(self, c=None, t=None, e=None):
        return (
            self.c if c is None else c,
            self.t if t is None else t,
            self.e if e is None else e,
        )

    def greet(self, ctx, group):
        barrier = pltpu.get_barrier_semaphore()
        total = 0
        if ctx:
            for k in range(1, self.n):
                pl.semaphore_signal(
                    barrier, 1, device_id=self.at(c=self.ctx_peer(k)), device_id_type=MESH
                )
            total += self.n - 1
        if group:
            for b in range(1, self.ep):
                pl.semaphore_signal(
                    barrier, 1, device_id=self.at(e=self.ep_peer(b)), device_id_type=MESH
                )
            pl.semaphore_signal(barrier, 1, device_id=self.at(t=1 - self.t), device_id_type=MESH)
            total += self.ep
        pl.semaphore_wait(barrier, total)


def remote(src, dst, send, recv, device):
    return pltpu.make_async_remote_copy(
        src_ref=src, dst_ref=dst, send_sem=send, recv_sem=recv, device_id=device, device_id_type=MESH
    )


def swiglu_tile(x_ref, y_ref, gate_ref, up_ref, down_ref, acc_ref, first):
    a = contract_last(x_ref[...], gate_ref[...])
    b = contract_last(x_ref[...], up_ref[...])
    back = contract_last(y_ref[...], down_ref[...])
    s = jax.nn.sigmoid(a)
    grad_a = (back * b * s * (1.0 + a * (1.0 - s))).astype(BF16)
    grad_b = (back * a * s).astype(BF16)
    width = acc_ref.shape[1]
    step = 512 if width % 512 == 0 else width
    for at in range(0, width, step):
        cols = pl.ds(at, step)
        term = jnp.dot(grad_a, gate_ref[:, cols], preferred_element_type=F32) + jnp.dot(
            grad_b, up_ref[:, cols], preferred_element_type=F32
        )

        @pl.when(first)
        def _():
            acc_ref[:, cols] = term

        @pl.when(jnp.logical_not(first))
        def _():
            acc_ref[:, cols] = acc_ref[:, cols] + term


def dispatch_kernel(
    dims, tiles, rows_ref, x_ref, y_ref, gate_ref, up_ref, down_ref,
    out_ref, part_ref, acc_ref, send1, recv1, send2, recv2, send3, recv3, local
):
    p = Place(*dims)
    step = pl.program_id(0)

    def across(k):
        d = p.ctx_peer(k)
        return remote(rows_ref.at[d], out_ref.at[p.t, p.e, p.c], send1.at[d], recv1.at[p.c], p.at(c=d))

    def arrive(src):
        return remote(
            rows_ref.at[src], out_ref.at[p.t, p.e, src], send1.at[src], recv1.at[src], p.at(c=src)
        )

    def to_ep(b, src, own):
        block = rows_ref.at[src] if own else out_ref.at[p.t, p.e, src]
        return remote(
            block, out_ref.at[p.t, p.e, src], send2.at[b, src], recv2.at[b, src], p.at(e=p.ep_peer(b))
        )

    def from_ep(b, src):
        e = p.ep_from(b)
        return remote(
            out_ref.at[p.t, e, src], out_ref.at[p.t, e, src], send2.at[b, src], recv2.at[b, src], p.at(e=e)
        )

    def to_core(e, src, own=False):
        block = rows_ref.at[src] if own else out_ref.at[p.t, e, src]
        return remote(
            block, out_ref.at[p.t, e, src], send3.at[e, src], recv3.at[e, src], p.at(t=1 - p.t)
        )

    def from_core(e, src):
        block = out_ref.at[1 - p.t, e, src]
        return remote(block, block, send3.at[e, src], recv3.at[e, src], p.at(t=1 - p.t))

    def keep():
        return pltpu.make_async_copy(rows_ref.at[p.c], out_ref.at[p.t, p.e, p.c], local)

    @pl.when(step == 0)
    def _():
        p.greet(True, True)

        @pl.loop(1, p.n)
        def _(k):
            across(k).start()

        for b in range(1, p.ep):
            to_ep(b, p.c, True).start()
        to_core(p.e, p.c, True).start()
        keep().start()

    swiglu_tile(x_ref, y_ref, gate_ref, up_ref, down_ref, acc_ref, step == 0)

    @pl.when(step == tiles - 1)
    def _():
        part_ref[...] = acc_ref[...].astype(BF16)

        def pass_on(src):
            for b in range(1, p.ep):
                from_ep(b, src).wait_recv()
                to_core(p.ep_from(b), src).start()

        @pl.loop(1, p.n)
        def _(k):
            src = p.ctx_from(k)
            arrive(src).wait_recv()
            for b in range(1, p.ep):
                to_ep(b, src, False).start()
            to_core(p.e, src).start()
            pass_on(p.ctx_from(k - 1))

        pass_on(p.ctx_from(p.n - 1))
        keep().wait()

        @pl.loop(0, p.n)
        def _(src):
            for e in range(p.ep):
                from_core(e, src).wait_recv()
                to_core(e, src).wait_send()
            for b in range(1, p.ep):
                to_ep(b, src, False).wait_send()

        @pl.loop(1, p.n)
        def _(k):
            across(k).wait_send()


def expert_kernel(
    dims, tiles, x_ref, y_ref, gate_ref, up_ref, down_ref, kvq_ref,
    out_ref, all_ref, acc_ref, send, recv, local
):
    p = Place(*dims)
    step = pl.program_id(0)

    def across(k):
        d = p.ctx_peer(k)
        return remote(kvq_ref, all_ref.at[p.c], send.at[d], recv.at[p.c], p.at(c=d))

    def arrive(src):
        return remote(kvq_ref, all_ref.at[src], send.at[src], recv.at[src], p.at(c=src))

    def keep():
        return pltpu.make_async_copy(kvq_ref, all_ref.at[p.c], local)

    @pl.when(step == 0)
    def _():
        p.greet(True, False)

        @pl.loop(1, p.n)
        def _(k):
            across(k).start()

        keep().start()

    swiglu_tile(x_ref, y_ref, gate_ref.at[0], up_ref.at[0], down_ref.at[0], acc_ref, step == 0)

    @pl.when(step == tiles - 1)
    def _():
        out_ref[...] = acc_ref[...].astype(BF16)
        keep().wait()

        @pl.loop(1, p.n)
        def _(k):
            arrive(p.ctx_from(k)).wait_recv()
            across(k).wait_send()


def return_kernel(
    dims, chunks, part_ref, back_ref, dense_ref,
    core_buf, ep_out, ep_in, fin_ref, send1, recv1, send2, recv2, send3, recv3
):
    p = Place(*dims)
    p.greet(True, True)

    def to_core(e, i):
        return remote(
            part_ref.at[1 - p.t, e, i], core_buf.at[e, i], send1.at[e, i], recv1.at[e, i], p.at(t=1 - p.t)
        )

    def to_ep(b, i):
        return remote(
            ep_out.at[b, i], ep_in.at[b, i], send2.at[b, i], recv2.at[b, i], p.at(e=p.ep_peer(b))
        )

    def home(d):
        return remote(fin_ref.at[d], back_ref.at[p.c], send3.at[d], recv3.at[p.c], p.at(c=d))

    def arrive(src):
        return remote(fin_ref.at[src], back_ref.at[src], send3.at[src], recv3.at[src], p.at(c=src))

    def chunk_of(k):
        return jnp.where(k < p.n, lax.rem(p.c + k + 1, p.n), k)

    @pl.loop(0, chunks)
    def _(k):
        i = chunk_of(k)
        for b in range(1, p.ep):
            to_core(p.ep_peer(b), i).start()
        to_core(p.e, i).start()

    @pl.loop(0, chunks)
    def _(k):
        i = chunk_of(k)
        for b in range(1, p.ep):
            e = p.ep_peer(b)
            to_core(e, i).wait_recv()
            ep_out[b, i] = (part_ref[p.t, e, i].astype(F32) + core_buf[e, i].astype(F32)).astype(BF16)
            to_ep(b, i).start()

    def total(i):
        to_core(p.e, i).wait_recv()
        value = part_ref[p.t, p.e, i].astype(F32) + core_buf[p.e, i].astype(F32)
        for b in range(1, p.ep):
            to_ep(b, i).wait_recv()
            value = value + ep_in[b, i].astype(F32)
        return value

    @pl.loop(0, p.n - 1)
    def _(k):
        i = chunk_of(k)
        fin_ref[i] = total(i).astype(BF16)
        home(i).start()

    back_ref[p.c] = total(p.c).astype(BF16)

    @pl.loop(p.n, chunks)
    def _(i):
        dense_ref[i - p.n] = total(i)

    @pl.loop(1, p.n)
    def _(k):
        arrive(p.ctx_from(k)).wait_recv()
        home(p.ctx_peer(k)).wait_send()

    @pl.loop(0, chunks)
    def _(i):
        for b in range(1, p.ep):
            to_ep(b, i).wait_send()
        for e in range(p.ep):
            to_core(e, i).wait_send()


def group_kernel(dims, own_ref, all_ref, send2, recv2, send3, recv3):
    p = Place(*dims)
    p.greet(False, True)
    all_ref[p.t, p.e] = own_ref[...]

    def to_ep(b):
        return remote(own_ref, all_ref.at[p.t, p.e], send2.at[b], recv2.at[b], p.at(e=p.ep_peer(b)))

    def from_ep(b):
        e = p.ep_from(b)
        return remote(own_ref, all_ref.at[p.t, e], send2.at[b], recv2.at[b], p.at(e=e))

    def to_core(e, own=False):
        block = own_ref if own else all_ref.at[p.t, e]
        return remote(block, all_ref.at[p.t, e], send3.at[e], recv3.at[e], p.at(t=1 - p.t))

    def from_core(e):
        block = all_ref.at[1 - p.t, e]
        return remote(block, block, send3.at[e], recv3.at[e], p.at(t=1 - p.t))

    for b in range(1, p.ep):
        to_ep(b).start()
    to_core(p.e, True).start()
    for b in range(1, p.ep):
        from_ep(b).wait_recv()
        to_core(p.ep_from(b)).start()
    for e in range(p.ep):
        from_core(e).wait_recv()
        to_core(e).wait_send()
    for b in range(1, p.ep):
        to_ep(b).wait_send()


def attention_kernel(
    dims, g_ref, kvq_ref, dq_ref, dk_ref, dv_ref, g_all, stats, mine, send1, recv1, send2, recv2
):
    p = Place(*dims)
    p.greet(True, False)
    n = p.n
    rows, width = g_ref.shape
    heads = width // HEAD_DIM
    seq = n * rows
    scale = HEAD_DIM ** (-0.5)

    def across(k):
        d = p.ctx_peer(k)
        return remote(g_ref, g_all.at[p.c], send1.at[d], recv1.at[p.c], p.at(c=d))

    def across_stats(k):
        d = p.ctx_peer(k)
        return remote(mine, stats.at[p.c], send2.at[d], recv2.at[p.c], p.at(c=d))

    def arrive(src):
        return remote(g_ref, g_all.at[src], send1.at[src], recv1.at[src], p.at(c=src))

    def arrive_stats(src):
        return remote(mine, stats.at[src], send2.at[src], recv2.at[src], p.at(c=src))

    @pl.loop(1, n)
    def _(k):
        across(k).start()

    g_all[p.c] = g_ref[...]
    mine[...] = jnp.zeros_like(mine)
    query_at = p.c * rows + lax.broadcasted_iota(jnp.int32, (rows, seq), 0)
    key_at = lax.broadcasted_iota(jnp.int32, (rows, seq), 1)
    allowed = key_at <= query_at
    for h in range(heads):
        cols = pl.ds(h * HEAD_DIM, HEAD_DIM)
        keys = kvq_ref[:, :, h * HEAD_DIM:(h + 1) * HEAD_DIM].reshape(seq, HEAD_DIM)
        values = kvq_ref[:, :, width + h * HEAD_DIM:width + (h + 1) * HEAD_DIM].reshape(seq, HEAD_DIM)
        q = kvq_ref[p.c, :, pl.ds(2 * width + h * HEAD_DIM, HEAD_DIM)]
        scores = jnp.where(allowed, contract_last(q, keys) * scale, NEG_FILL)
        top = jnp.max(scores, axis=1, keepdims=True)
        weights = jnp.where(allowed, jnp.exp(scores - top), 0.0)
        total = jnp.sum(weights, axis=1, keepdims=True)
        probs = weights / total
        grad_probs = contract_last(g_ref[:, cols], values)
        delta = jnp.sum(probs * grad_probs, axis=1, keepdims=True)
        log_norm = top + jnp.log(total)
        mine[h:h + 1, :] = jnp.transpose(jnp.broadcast_to(delta, (rows, 128)))[0:1, :]
        mine[heads + h:heads + h + 1, :] = jnp.transpose(jnp.broadcast_to(log_norm, (rows, 128)))[0:1, :]
        grad_scores = (probs * (grad_probs - delta)).astype(BF16)
        dq_ref[:, cols] = (jnp.dot(grad_scores, keys, preferred_element_type=F32) * scale).astype(BF16)

    @pl.loop(1, n)
    def _(k):
        across_stats(k).start()

    stats[p.c] = mine[...]

    @pl.loop(1, n)
    def _(k):
        arrive(p.ctx_from(k)).wait_recv()
        arrive_stats(p.ctx_from(k)).wait_recv()

    key_at = p.c * rows + lax.broadcasted_iota(jnp.int32, (rows, seq), 0)
    query_at = lax.broadcasted_iota(jnp.int32, (rows, seq), 1)
    allowed = key_at <= query_at
    for h in range(heads):
        cols = pl.ds(h * HEAD_DIM, HEAD_DIM)
        queries = kvq_ref[:, :, 2 * width + h * HEAD_DIM:2 * width + (h + 1) * HEAD_DIM].reshape(
            seq, HEAD_DIM
        )
        upstream = g_all[:, :, h * HEAD_DIM:(h + 1) * HEAD_DIM].reshape(seq, HEAD_DIM)
        keys = kvq_ref[p.c, :, pl.ds(h * HEAD_DIM, HEAD_DIM)]
        values = kvq_ref[p.c, :, pl.ds(width + h * HEAD_DIM, HEAD_DIM)]
        delta = jnp.concatenate([stats[s, h:h + 1, :] for s in range(n)], axis=1)
        log_norm = jnp.concatenate([stats[s, heads + h:heads + h + 1, :] for s in range(n)], axis=1)
        scores = contract_last(keys, queries) * scale
        probs = jnp.where(allowed, jnp.exp(jnp.where(allowed, scores - log_norm, 0.0)), 0.0)
        grad_scores = (probs * (contract_last(values, upstream) - delta)).astype(BF16)
        dv_ref[:, cols] = jnp.dot(probs.astype(BF16), upstream, preferred_element_type=F32).astype(BF16)
        dk_ref[:, cols] = (jnp.dot(grad_scores, queries, preferred_element_type=F32) * scale).astype(BF16)

    @pl.loop(1, n)
    def _(k):
        across(k).wait_send()
        across_stats(k).wait_send()


def params(collective_id, grid=False):
    return pltpu.CompilerParams(
        collective_id=collective_id,
        has_side_effects=True,
        vmem_limit_bytes=56 * 1024 * 1024,
        **({"dimension_semantics": ("arbitrary",)} if grid else {}),
    )


def body(
    dims, hidden, grad_out, gain, dense_gate, dense_up, dense_down, expert_gate, expert_up, expert_down,
    out_proj, queries, keys, values, route_ids, route_weights
):
    n, tp, ep = dims
    group = tp * ep
    rows, width = hidden.shape
    part = width // group
    picks = route_ids.shape[1]
    capacity = 5 * rows // (2 * n)
    pair = round_up(2 * capacity, 16)
    chunk = round_up(capacity, 16)
    sem = pltpu.SemaphoreType.DMA
    at = lax.axis_index("tp") * ep + lax.axis_index("ep")

    hidden_f = hidden.astype(F32)
    inverse = lax.rsqrt(jnp.mean(hidden_f * hidden_f, axis=1, keepdims=True) + EPSILON)
    normed = hidden_f * inverse
    mixed_in = (normed * gain).astype(BF16)

    flat_ids = route_ids.reshape(-1)
    hits = (flat_ids[:, None] == lax.iota(jnp.int32, n)[None, :]).astype(BF16)
    order = lax.iota(jnp.int32, picks * rows)
    before = (order[None, :] < order[:, None]).astype(BF16)
    earlier = jnp.dot(before, hits, preferred_element_type=F32)
    slots = jnp.sum(earlier * hits.astype(F32), axis=1).astype(jnp.int32)
    slots = slots.reshape(rows, picks)
    pair_at = (route_ids * pair + slots).T
    home_at = route_ids * chunk + slots
    places = lax.iota(jnp.int32, n * pair)[:, None]
    own_in = lax.dynamic_slice(mixed_in, (0, at * part), (rows, part))
    own_out = lax.dynamic_slice(grad_out, (0, at * part), (rows, part))
    pick_in = sum((places == pair_at[k][None, :]).astype(BF16) for k in range(picks))
    pick_out = [(places == pair_at[k][None, :] + capacity) for k in range(picks)]
    weight_of = sum(
        jnp.sum(jnp.where(pick_out[k], route_weights[:, k][None, :], 0.0), axis=1, keepdims=True)
        for k in range(picks)
    )
    pick_out = sum(hit.astype(BF16) for hit in pick_out)
    send_rows = (
        jnp.dot(pick_in, own_in, preferred_element_type=F32)
        + jnp.dot(pick_out, own_out, preferred_element_type=F32) * weight_of
    ).astype(BF16).reshape(n, pair, part)

    ff = dense_gate.shape[0]
    ff_tile = tile_of(ff, 320)
    weight_spec = pl.BlockSpec((ff_tile, width), lambda i: (i, 0))
    full = pl.BlockSpec((rows, width), lambda i: (0, 0))
    arrived, dense_part = pl.pallas_call(
        functools.partial(dispatch_kernel, dims, ff // ff_tile),
        grid=(ff // ff_tile,),
        out_shape=(
            jax.ShapeDtypeStruct((tp, ep, n, pair, part), BF16),
            jax.ShapeDtypeStruct((rows, width), BF16),
        ),
        in_specs=[ANY, full, full, weight_spec, weight_spec, weight_spec],
        out_specs=(ANY, full),
        scratch_shapes=[pltpu.VMEM((rows, width), F32)]
        + [sem((n,))] * 2 + [sem((ep, n))] * 4 + [sem],
        compiler_params=params(1, True),
        name="dispatch_dense",
    )(send_rows, mixed_in, grad_out, dense_gate, dense_up, dense_down)

    arrived = arrived.reshape(group, n, pair, part)

    def joined(low):
        return arrived[:, :, low:low + capacity].transpose(1, 2, 0, 3).reshape(n * capacity, width)

    kvq = jnp.concatenate([keys, values, queries], axis=1)
    head_width = queries.shape[1]
    eh = expert_gate.shape[1]
    eh_tile = tile_of(eh, 320)
    weight_spec = pl.BlockSpec((1, eh_tile, width), lambda i: (0, i, 0))
    full = pl.BlockSpec((n * capacity, width), lambda i: (0, 0))
    expert_part, kvq_all = pl.pallas_call(
        functools.partial(expert_kernel, dims, eh // eh_tile),
        grid=(eh // eh_tile,),
        out_shape=(
            jax.ShapeDtypeStruct((n * capacity, width), BF16),
            jax.ShapeDtypeStruct((n, rows, 3 * head_width), BF16),
        ),
        in_specs=[full, full, weight_spec, weight_spec, weight_spec, ANY],
        out_specs=(full, ANY),
        scratch_shapes=[pltpu.VMEM((n * capacity, width), F32)] + [sem((n,))] * 2 + [sem],
        compiler_params=params(2, True),
        name="expert_gather",
    )(joined(0), joined(capacity), expert_gate, expert_up, expert_down, kvq)

    dense_chunks = -(-rows // chunk)
    chunks = n + dense_chunks
    expert_part = jnp.pad(
        expert_part.reshape(n, capacity, group, part), ((0, 0), (0, chunk - capacity), (0, 0), (0, 0))
    )
    dense_part = jnp.pad(
        dense_part.reshape(rows, group, part), ((0, dense_chunks * chunk - rows), (0, 0), (0, 0))
    ).reshape(dense_chunks, chunk, group, part)
    parts = jnp.concatenate([expert_part, dense_part], axis=0).transpose(2, 0, 1, 3)
    parts = parts.reshape(tp, ep, chunks, chunk, part)
    returned, dense_sum = pl.pallas_call(
        functools.partial(return_kernel, dims, chunks),
        out_shape=(
            jax.ShapeDtypeStruct((n, chunk, part), BF16),
            jax.ShapeDtypeStruct((dense_chunks, chunk, part), F32),
        ),
        in_specs=[WHOLE],
        out_specs=(WHOLE, WHOLE),
        scratch_shapes=[
            pltpu.VMEM((ep, chunks, chunk, part), BF16),
            pltpu.VMEM((ep, chunks, chunk, part), BF16),
            pltpu.VMEM((ep, chunks, chunk, part), BF16),
            pltpu.VMEM((n, chunk, part), BF16),
        ]
        + [sem((ep, chunks))] * 4 + [sem((n,))] * 2,
        compiler_params=params(3),
        name="return_rows",
    )(parts)

    home_places = lax.iota(jnp.int32, n * chunk)[None, :]
    take = sum((home_places == home_at[:, k:k + 1]).astype(BF16) for k in range(picks))
    own_total = (
        jnp.dot(take, returned.reshape(n * chunk, part), preferred_element_type=F32)
        + dense_sum.reshape(dense_chunks * chunk, part)[:rows]
    ).astype(BF16)
    total_grad = pl.pallas_call(
        functools.partial(group_kernel, dims),
        out_shape=jax.ShapeDtypeStruct((tp, ep, rows, part), BF16),
        in_specs=[WHOLE],
        out_specs=WHOLE,
        scratch_shapes=[sem((ep,))] * 4,
        compiler_params=params(4),
        name="group_gather",
    )(own_total)
    total_grad = total_grad.reshape(group, rows, part).transpose(1, 0, 2).reshape(rows, width).astype(F32)
    scaled_grad = total_grad * gain
    grad_hidden = (
        grad_out.astype(F32)
        + inverse * (scaled_grad - normed * jnp.mean(scaled_grad * normed, axis=1, keepdims=True))
    ).astype(BF16)
    grad_heads = contract_last(grad_hidden, out_proj).astype(BF16)

    heads = head_width // HEAD_DIM
    stat_rows = round_up(2 * heads, 8)
    grads = jax.ShapeDtypeStruct((rows, head_width), BF16)
    grad_queries, grad_keys, grad_values = pl.pallas_call(
        functools.partial(attention_kernel, dims),
        out_shape=(grads, grads, grads),
        in_specs=[WHOLE, WHOLE],
        out_specs=(WHOLE, WHOLE, WHOLE),
        scratch_shapes=[
            pltpu.VMEM((n, rows, head_width), BF16),
            pltpu.VMEM((n, stat_rows, rows), F32),
            pltpu.VMEM((stat_rows, rows), F32),
        ]
        + [sem((n,))] * 4,
        compiler_params=params(5),
        name="attention_grads",
    )(grad_heads, kvq_all)
    return (grad_hidden, grad_queries, grad_keys, grad_values)


def solution(mesh):
    dims = (mesh.shape["ctx"], mesh.shape["tp"], mesh.shape["ep"])
    hidden_units = P(("tp", "ep"), None)
    expert_units = P("ctx", ("tp", "ep"), None)
    by_head = P("ctx", ("tp", "ep"))
    return jax.shard_map(
        functools.partial(body, dims),
        mesh=mesh,
        in_specs=(
            P("ctx", None), P("ctx", None), P(),
            hidden_units, hidden_units, hidden_units,
            expert_units, expert_units, expert_units,
            hidden_units, by_head, by_head, by_head,
            P("ctx", None), P("ctx", None),
        ),
        out_specs=(P("ctx", None), by_head, by_head, by_head),
        check_vma=False,
    )
```

```python
import functools

import jax
import jax.numpy as jnp
from jax import lax
from jax.experimental import pallas as pl
from jax.experimental.pallas import tpu as pltpu
from jax.sharding import PartitionSpec as P

HEAD_DIM = 128
NEG_FILL = -1e30
EPSILON = 1e-05
MESH = pl.DeviceIdType.MESH
ANY = pl.BlockSpec(memory_space=pl.ANY)
WHOLE = pl.BlockSpec(memory_space=pltpu.VMEM)
BF16 = jnp.bfloat16
F32 = jnp.float32


def contract_last(left_rows, right_rows):
    return lax.dot_general(
        left_rows, right_rows, (((1,), (1,)), ((), ())), preferred_element_type=F32
    )


def round_up(value, step):
    return -(-value // step) * step


def tile_of(hidden, most):
    fits = [t for t in range(16, most + 1, 16) if hidden % t == 0]
    return max(fits) if fits else hidden


class Place:
    def __init__(self, n, tp, ep):
        self.n, self.tp, self.ep = n, tp, ep
        self.c = lax.axis_index("ctx")
        self.t = lax.axis_index("tp")
        self.e = lax.axis_index("ep")

    def ctx_peer(self, k):
        return lax.rem(self.c + k, self.n)

    def ctx_from(self, k):
        return lax.rem(self.c + self.n - k, self.n)

    def ep_peer(self, b):
        return lax.rem(self.e + b, self.ep)

    def ep_from(self, b):
        return lax.rem(self.e + self.ep - b, self.ep)

    def at(self, c=None, t=None, e=None):
        return (
            self.c if c is None else c,
            self.t if t is None else t,
            self.e if e is None else e,
        )

    def greet(self, ctx, group):
        barrier = pltpu.get_barrier_semaphore()
        total = 0
        if ctx:
            for k in range(1, self.n):
                pl.semaphore_signal(
                    barrier, 1, device_id=self.at(c=self.ctx_peer(k)), device_id_type=MESH
                )
            total += self.n - 1
        if group:
            for b in range(1, self.ep):
                pl.semaphore_signal(
                    barrier, 1, device_id=self.at(e=self.ep_peer(b)), device_id_type=MESH
                )
            pl.semaphore_signal(barrier, 1, device_id=self.at(t=1 - self.t), device_id_type=MESH)
            total += self.ep
        pl.semaphore_wait(barrier, total)


def remote(src, dst, send, recv, device):
    return pltpu.make_async_remote_copy(
        src_ref=src, dst_ref=dst, send_sem=send, recv_sem=recv, device_id=device, device_id_type=MESH
    )


def swiglu_tile(x_ref, y_ref, gate_ref, up_ref, down_ref, acc_ref, first):
    a = contract_last(x_ref[...], gate_ref[...])
    b = contract_last(x_ref[...], up_ref[...])
    back = contract_last(y_ref[...], down_ref[...])
    s = jax.nn.sigmoid(a)
    grad_a = (back * b * s * (1.0 + a * (1.0 - s))).astype(BF16)
    grad_b = (back * a * s).astype(BF16)
    width = acc_ref.shape[1]
    step = 512 if width % 512 == 0 else width
    for at in range(0, width, step):
        cols = pl.ds(at, step)
        term = jnp.dot(grad_a, gate_ref[:, cols], preferred_element_type=F32) + jnp.dot(
            grad_b, up_ref[:, cols], preferred_element_type=F32
        )

        @pl.when(first)
        def _():
            acc_ref[:, cols] = term

        @pl.when(jnp.logical_not(first))
        def _():
            acc_ref[:, cols] = acc_ref[:, cols] + term


def dispatch_kernel(
    dims, tiles, rows_ref, x_ref, y_ref, gate_ref, up_ref, down_ref,
    out_ref, part_ref, acc_ref, send1, recv1, send2, recv2, send3, recv3, local
):
    p = Place(*dims)
    step = pl.program_id(0)

    def across(k):
        d = p.ctx_peer(k)
        return remote(rows_ref.at[d], out_ref.at[p.t, p.e, p.c], send1.at[d], recv1.at[p.c], p.at(c=d))

    def arrive(src):
        return remote(
            rows_ref.at[src], out_ref.at[p.t, p.e, src], send1.at[src], recv1.at[src], p.at(c=src)
        )

    def to_ep(b, src, own):
        block = rows_ref.at[src] if own else out_ref.at[p.t, p.e, src]
        return remote(
            block, out_ref.at[p.t, p.e, src], send2.at[b, src], recv2.at[b, src], p.at(e=p.ep_peer(b))
        )

    def from_ep(b, src):
        e = p.ep_from(b)
        return remote(
            out_ref.at[p.t, e, src], out_ref.at[p.t, e, src], send2.at[b, src], recv2.at[b, src], p.at(e=e)
        )

    def to_core(e, src, own=False):
        block = rows_ref.at[src] if own else out_ref.at[p.t, e, src]
        return remote(
            block, out_ref.at[p.t, e, src], send3.at[e, src], recv3.at[e, src], p.at(t=1 - p.t)
        )

    def from_core(e, src):
        block = out_ref.at[1 - p.t, e, src]
        return remote(block, block, send3.at[e, src], recv3.at[e, src], p.at(t=1 - p.t))

    def keep():
        return pltpu.make_async_copy(rows_ref.at[p.c], out_ref.at[p.t, p.e, p.c], local)

    @pl.when(step == 0)
    def _():
        p.greet(True, True)

        @pl.loop(1, p.n)
        def _(k):
            across(k).start()

        for b in range(1, p.ep):
            to_ep(b, p.c, True).start()
        to_core(p.e, p.c, True).start()
        keep().start()

    swiglu_tile(x_ref, y_ref, gate_ref, up_ref, down_ref, acc_ref, step == 0)

    @pl.when(step == tiles - 1)
    def _():
        part_ref[...] = acc_ref[...].astype(BF16)

        def pass_on(src):
            for b in range(1, p.ep):
                from_ep(b, src).wait_recv()
                to_core(p.ep_from(b), src).start()

        @pl.loop(1, p.n)
        def _(k):
            src = p.ctx_from(k)
            arrive(src).wait_recv()
            for b in range(1, p.ep):
                to_ep(b, src, False).start()
            to_core(p.e, src).start()
            pass_on(p.ctx_from(k - 1))

        pass_on(p.ctx_from(p.n - 1))
        keep().wait()

        @pl.loop(0, p.n)
        def _(src):
            for e in range(p.ep):
                from_core(e, src).wait_recv()
                to_core(e, src).wait_send()
            for b in range(1, p.ep):
                to_ep(b, src, False).wait_send()

        @pl.loop(1, p.n)
        def _(k):
            across(k).wait_send()


def expert_kernel(
    dims, tiles, x_ref, y_ref, gate_ref, up_ref, down_ref, kvq_ref,
    out_ref, all_ref, acc_ref, send, recv, local
):
    p = Place(*dims)
    step = pl.program_id(0)

    def across(k):
        d = p.ctx_peer(k)
        return remote(kvq_ref, all_ref.at[p.c], send.at[d], recv.at[p.c], p.at(c=d))

    def arrive(src):
        return remote(kvq_ref, all_ref.at[src], send.at[src], recv.at[src], p.at(c=src))

    def keep():
        return pltpu.make_async_copy(kvq_ref, all_ref.at[p.c], local)

    @pl.when(step == 0)
    def _():
        p.greet(True, False)

        @pl.loop(1, p.n)
        def _(k):
            across(k).start()

        keep().start()

    swiglu_tile(x_ref, y_ref, gate_ref.at[0], up_ref.at[0], down_ref.at[0], acc_ref, step == 0)

    @pl.when(step == tiles - 1)
    def _():
        out_ref[...] = acc_ref[...].astype(BF16)
        keep().wait()

        @pl.loop(1, p.n)
        def _(k):
            arrive(p.ctx_from(k)).wait_recv()
            across(k).wait_send()


def return_kernel(
    dims, chunks, part_ref, back_ref, dense_ref,
    core_buf, ep_out, ep_in, fin_ref, send1, recv1, send2, recv2, send3, recv3
):
    p = Place(*dims)
    p.greet(True, True)

    def to_core(e, i):
        return remote(
            part_ref.at[1 - p.t, e, i], core_buf.at[e, i], send1.at[e, i], recv1.at[e, i], p.at(t=1 - p.t)
        )

    def to_ep(b, i):
        return remote(
            ep_out.at[b, i], ep_in.at[b, i], send2.at[b, i], recv2.at[b, i], p.at(e=p.ep_peer(b))
        )

    def home(d):
        return remote(fin_ref.at[d], back_ref.at[p.c], send3.at[d], recv3.at[p.c], p.at(c=d))

    def arrive(src):
        return remote(fin_ref.at[src], back_ref.at[src], send3.at[src], recv3.at[src], p.at(c=src))

    def chunk_of(k):
        return jnp.where(k < p.n, lax.rem(p.c + k + 1, p.n), k)

    @pl.loop(0, chunks)
    def _(k):
        i = chunk_of(k)
        for b in range(1, p.ep):
            to_core(p.ep_peer(b), i).start()
        to_core(p.e, i).start()

    @pl.loop(0, chunks)
    def _(k):
        i = chunk_of(k)
        for b in range(1, p.ep):
            e = p.ep_peer(b)
            to_core(e, i).wait_recv()
            ep_out[b, i] = (part_ref[p.t, e, i].astype(F32) + core_buf[e, i].astype(F32)).astype(BF16)
            to_ep(b, i).start()

    def total(i):
        to_core(p.e, i).wait_recv()
        value = part_ref[p.t, p.e, i].astype(F32) + core_buf[p.e, i].astype(F32)
        for b in range(1, p.ep):
            to_ep(b, i).wait_recv()
            value = value + ep_in[b, i].astype(F32)
        return value

    @pl.loop(0, p.n - 1)
    def _(k):
        i = chunk_of(k)
        fin_ref[i] = total(i).astype(BF16)
        home(i).start()

    back_ref[p.c] = total(p.c).astype(BF16)

    @pl.loop(p.n, chunks)
    def _(i):
        dense_ref[i - p.n] = total(i)

    @pl.loop(1, p.n)
    def _(k):
        arrive(p.ctx_from(k)).wait_recv()
        home(p.ctx_peer(k)).wait_send()

    @pl.loop(0, chunks)
    def _(i):
        for b in range(1, p.ep):
            to_ep(b, i).wait_send()
        for e in range(p.ep):
            to_core(e, i).wait_send()


def experts_kernel(
    dims, capacity, rows_ref, x_ref, y_ref, dense_gate, dense_up, dense_down,
    expert_gate, expert_up, expert_down, kvq_ref, back_ref, dense_ref, all_ref,
    got, x_in, y_in, weights, grad_a, grad_b, out, core_buf, ep_out, ep_in, fin_ref,
    send1, recv1, send2, recv2, send3, recv3, send4, recv4, send5, recv5, send6, recv6,
    send7, recv7, send8, recv8, loads, local
):
    p = Place(*dims)
    n = p.n
    part = rows_ref.shape[2]
    rows, width = x_ref.shape
    ff, eh = dense_gate.shape[0], expert_gate.shape[1]
    chunks, chunk = out.shape[0], out.shape[1]
    head_width = kvq_ref.shape[1] // 3

    def cols(t, e):
        return pl.ds(pl.multiple_of((t * p.ep + e) * part, 128), part)

    def across(k):
        d = p.ctx_peer(k)
        return remote(
            rows_ref.at[d], got.at[p.c, :, cols(p.t, p.e)], send1.at[d], recv1.at[p.c], p.at(c=d)
        )

    def arrive(src):
        return remote(
            rows_ref.at[src], got.at[src, :, cols(p.t, p.e)], send1.at[src], recv1.at[src], p.at(c=src)
        )

    def to_ep(b, src, own=False):
        slot = got.at[src, :, cols(p.t, p.e)]
        return remote(
            rows_ref.at[src] if own else slot, slot, send2.at[b, src], recv2.at[b, src],
            p.at(e=p.ep_peer(b)),
        )

    def from_ep(b, src):
        e = p.ep_from(b)
        slot = got.at[src, :, cols(p.t, e)]
        return remote(slot, slot, send2.at[b, src], recv2.at[b, src], p.at(e=e))

    def to_core(e, src, own=False):
        slot = got.at[src, :, cols(p.t, e)]
        return remote(
            rows_ref.at[src] if own else slot, slot, send3.at[e, src], recv3.at[e, src], p.at(t=1 - p.t)
        )

    def from_core(e, src):
        slot = got.at[src, :, cols(1 - p.t, e)]
        return remote(slot, slot, send3.at[e, src], recv3.at[e, src], p.at(t=1 - p.t))

    def keep():
        return pltpu.make_async_copy(rows_ref.at[p.c], got.at[p.c, :, cols(p.t, p.e)], local.at[0])

    def pass_on(src):
        for b in range(1, p.ep):
            from_ep(b, src).wait_recv()
            to_core(p.ep_from(b), src).start()

    def forward(k):
        src = p.ctx_from(k)
        arrive(src).wait_recv()
        for b in range(1, p.ep):
            to_ep(b, src).start()
        to_core(p.e, src).start()
        pass_on(p.ctx_from(k - 1))

    def sum_core(e, i):
        return remote(
            out.at[i, :, cols(1 - p.t, e)], core_buf.at[e, i], send4.at[e, i], recv4.at[e, i],
            p.at(t=1 - p.t),
        )

    def sum_ep(b, i):
        return remote(
            ep_out.at[b - 1, i], ep_in.at[b - 1, i], send5.at[b, i], recv5.at[b, i], p.at(e=p.ep_peer(b))
        )

    def pass_sum(b, i):
        e = p.ep_peer(b)
        sum_core(e, i).wait_recv()
        ep_out[b - 1, i] = (out[i, :, cols(p.t, e)].astype(F32) + core_buf[e, i].astype(F32)).astype(BF16)
        sum_ep(b, i).start()

    def total(i):
        sum_core(p.e, i).wait_recv()
        value = out[i, :, cols(p.t, p.e)].astype(F32) + core_buf[p.e, i].astype(F32)
        for b in range(1, p.ep):
            sum_ep(b, i).wait_recv()
            value = value + ep_in[b - 1, i].astype(F32)
        return value

    def home(d):
        return remote(fin_ref.at[d], back_ref.at[p.c], send6.at[d], recv6.at[p.c], p.at(c=d))

    def home_from(src):
        return remote(fin_ref.at[src], back_ref.at[src], send6.at[src], recv6.at[src], p.at(c=src))

    def keys_to(d):
        at = pl.ds(0, 2 * head_width)
        return remote(
            kvq_ref.at[:, at], all_ref.at[p.c, :, at], send7.at[d], recv7.at[p.c], p.at(c=d)
        )

    def keys_from(src):
        at = pl.ds(0, 2 * head_width)
        return remote(
            kvq_ref.at[:, at], all_ref.at[src, :, at], send7.at[src], recv7.at[src], p.at(c=src)
        )

    def queries_to(d):
        at = pl.ds(2 * head_width, head_width)
        return remote(
            kvq_ref.at[:, at], all_ref.at[p.c, :, at], send8.at[d], recv8.at[p.c], p.at(c=d)
        )

    def queries_from(src):
        at = pl.ds(2 * head_width, head_width)
        return remote(
            kvq_ref.at[:, at], all_ref.at[src, :, at], send8.at[src], recv8.at[src], p.at(c=src)
        )

    def keep_kvq():
        return pltpu.make_async_copy(kvq_ref, all_ref.at[p.c], local.at[1])

    def load(j, ref, size):
        return pltpu.make_async_copy(ref, weights.at[j, pl.ds(0, size)], loads.at[j])

    dense = [load(j, ref, ff) for j, ref in enumerate((dense_gate, dense_up, dense_down))]
    expert = [
        load(j, ref.at[0], eh) for j, ref in enumerate((expert_gate, expert_up, expert_down))
    ]
    for copy in dense:
        copy.start()
    p.greet(True, True)

    @pl.loop(1, n)
    def _(k):
        across(k).start()

    for b in range(1, p.ep):
        to_ep(b, p.c, True).start()
    to_core(p.e, p.c, True).start()
    keep().start()
    keep_kvq().start()

    def slopes(a, b, back):
        s = jax.nn.sigmoid(a)
        return (back * b * s * (1.0 + a * (1.0 - s))).astype(BF16), (back * a * s).astype(BF16)

    for copy in dense:
        copy.wait()
    da, db = slopes(
        contract_last(x_ref[...], weights[0, 0:ff, :]),
        contract_last(x_ref[...], weights[1, 0:ff, :]),
        contract_last(y_ref[...], weights[2, 0:ff, :]),
    )
    step = 512 if width % 512 == 0 else width
    for low in range(0, width, step):
        term = jnp.dot(da, weights[0, 0:ff, low:low + step], preferred_element_type=F32) + jnp.dot(
            db, weights[1, 0:ff, low:low + step], preferred_element_type=F32
        )
        for j in range(chunks - n):
            piece = term[j * chunk:min((j + 1) * chunk, rows)]
            if piece.shape[0] < chunk:
                piece = jnp.concatenate(
                    [piece, jnp.zeros((chunk - piece.shape[0], step), F32)], axis=0
                )
            out[n + j, :, low:low + step] = piece.astype(BF16)
    for copy in expert:
        copy.start()

    @pl.loop(n, chunks)
    def _(i):
        for e in range(p.ep):
            sum_core(e, i).start()

    @pl.loop(1, n)
    def _(k):
        forward(k)

    pass_on(p.ctx_from(n - 1))
    keep().wait()

    @pl.loop(1, n)
    def _(k):
        @pl.when(p.c + k < n)
        def _():
            keys_to(p.c + k).start()

        @pl.when(p.c - k >= 0)
        def _():
            queries_to(p.c - k).start()

    for k in range(n):
        src = p.ctx_from(k)
        for e in range(p.ep):
            from_core(e, src).wait_recv()
        x_in[k * capacity:(k + 1) * capacity, :] = got[src, 0:capacity, :]
        y_in[k * capacity:(k + 1) * capacity, :] = got[src, capacity:2 * capacity, :]

    for copy in expert:
        copy.wait()
    for low in range(0, eh, 256):
        high = min(low + 256, eh)
        ga, gb = slopes(
            contract_last(x_in[...], weights[0, low:high, :]),
            contract_last(x_in[...], weights[1, low:high, :]),
            contract_last(y_in[...], weights[2, low:high, :]),
        )
        grad_a[:, low:high] = ga
        grad_b[:, low:high] = gb
        if low == 0:

            @pl.loop(n, chunks)
            def _(i):
                for b in range(1, p.ep):
                    pass_sum(b, i)

    def chunk_of(k):
        return lax.rem(p.c + k + 1, n)

    for mine in (False, True):
        for b in list(range(1, p.ep)) + [0]:
            t, e = (p.t if mine else 1 - p.t), p.ep_peer(b)
            value = jnp.dot(grad_a[...], weights[0, 0:eh, cols(t, e)], preferred_element_type=F32) + jnp.dot(
                grad_b[...], weights[1, 0:eh, cols(t, e)], preferred_element_type=F32
            )
            for k in range(n):
                piece = jnp.concatenate(
                    [value[k * capacity:(k + 1) * capacity], jnp.zeros((chunk - capacity, part), F32)],
                    axis=0,
                )
                out[p.ctx_from(k), :, cols(t, e)] = piece.astype(BF16)
            if not mine:

                @pl.loop(0, n)
                def _(k):
                    sum_core(e, chunk_of(k)).start()

            elif b:

                @pl.loop(0, n)
                def _(k):
                    pass_sum(b, chunk_of(k))

    @pl.loop(0, n - 1)
    def _(k):
        i = chunk_of(k)
        fin_ref[i] = total(i).astype(BF16)
        home(i).start()

    back_ref[p.c] = total(p.c).astype(BF16)

    @pl.loop(n, chunks)
    def _(i):
        dense_ref[i - n] = total(i)

    keep_kvq().wait()

    @pl.loop(1, n)
    def _(k):
        @pl.when(p.c + k < n)
        def _():
            keys_to(p.c + k).wait_send()
            queries_from(p.c + k).wait_recv()

        @pl.when(p.c - k >= 0)
        def _():
            queries_to(p.c - k).wait_send()
            keys_from(p.c - k).wait_recv()

        across(k).wait_send()
        home(p.ctx_peer(k)).wait_send()
        home_from(p.ctx_from(k)).wait_recv()

    @pl.loop(0, n)
    def _(src):
        for e in range(p.ep):
            to_core(e, src).wait_send()
        for b in range(1, p.ep):
            to_ep(b, src).wait_send()

    @pl.loop(0, chunks)
    def _(i):
        for e in range(p.ep):
            sum_core(e, i).wait_send()
        for b in range(1, p.ep):
            sum_ep(b, i).wait_send()


def group_kernel(dims, own_ref, all_ref, send2, recv2, send3, recv3):
    p = Place(*dims)
    p.greet(False, True)
    all_ref[p.t, p.e] = own_ref[...]

    def to_ep(b):
        return remote(own_ref, all_ref.at[p.t, p.e], send2.at[b], recv2.at[b], p.at(e=p.ep_peer(b)))

    def from_ep(b):
        e = p.ep_from(b)
        return remote(own_ref, all_ref.at[p.t, e], send2.at[b], recv2.at[b], p.at(e=e))

    def to_core(e, own=False):
        block = own_ref if own else all_ref.at[p.t, e]
        return remote(block, all_ref.at[p.t, e], send3.at[e], recv3.at[e], p.at(t=1 - p.t))

    def from_core(e):
        block = all_ref.at[1 - p.t, e]
        return remote(block, block, send3.at[e], recv3.at[e], p.at(t=1 - p.t))

    for b in range(1, p.ep):
        to_ep(b).start()
    to_core(p.e, True).start()
    for b in range(1, p.ep):
        from_ep(b).wait_recv()
        to_core(p.ep_from(b)).start()
    for e in range(p.ep):
        from_core(e).wait_recv()
        to_core(e).wait_send()
    for b in range(1, p.ep):
        to_ep(b).wait_send()


def attention_kernel(
    dims, g_ref, kvq_ref, dq_ref, dk_ref, dv_ref, g_all, stats, mine, send1, recv1, send2, recv2
):
    p = Place(*dims)
    p.greet(True, False)
    n = p.n
    rows, width = g_ref.shape
    heads = width // HEAD_DIM
    seq = n * rows
    scale = HEAD_DIM ** (-0.5)

    def across(d):
        return remote(g_ref, g_all.at[p.c], send1.at[d], recv1.at[p.c], p.at(c=d))

    def across_stats(d):
        return remote(mine, stats.at[p.c], send2.at[d], recv2.at[p.c], p.at(c=d))

    def arrive(src):
        return remote(g_ref, g_all.at[src], send1.at[src], recv1.at[src], p.at(c=src))

    def arrive_stats(src):
        return remote(mine, stats.at[src], send2.at[src], recv2.at[src], p.at(c=src))

    @pl.loop(1, n)
    def _(k):
        @pl.when(p.c - k >= 0)
        def _():
            across(p.c - k).start()

    g_all[p.c] = g_ref[...]
    mine[...] = jnp.zeros_like(mine)
    token = lax.broadcasted_iota(jnp.int32, (seq, HEAD_DIM), 0)
    early = token < (p.c + 1) * rows
    late = token >= p.c * rows
    nothing = jnp.zeros((seq, HEAD_DIM), BF16)
    query_at = p.c * rows + lax.broadcasted_iota(jnp.int32, (rows, seq), 0)
    key_at = lax.broadcasted_iota(jnp.int32, (rows, seq), 1)
    allowed = key_at <= query_at
    for h in range(heads):
        cols = pl.ds(h * HEAD_DIM, HEAD_DIM)
        keys = kvq_ref[:, :, h * HEAD_DIM:(h + 1) * HEAD_DIM].reshape(seq, HEAD_DIM)
        values = kvq_ref[:, :, width + h * HEAD_DIM:width + (h + 1) * HEAD_DIM].reshape(seq, HEAD_DIM)
        keys = jnp.where(early, keys, nothing)
        values = jnp.where(early, values, nothing)
        q = kvq_ref[p.c, :, pl.ds(2 * width + h * HEAD_DIM, HEAD_DIM)]
        scores = jnp.where(allowed, contract_last(q, keys) * scale, NEG_FILL)
        top = jnp.max(scores, axis=1, keepdims=True)
        weights = jnp.where(allowed, jnp.exp(scores - top), 0.0)
        total = jnp.sum(weights, axis=1, keepdims=True)
        probs = weights / total
        grad_probs = contract_last(g_ref[:, cols], values)
        delta = jnp.sum(probs * grad_probs, axis=1, keepdims=True)
        log_norm = top + jnp.log(total)
        mine[h:h + 1, :] = jnp.transpose(jnp.broadcast_to(delta, (rows, 128)))[0:1, :]
        mine[heads + h:heads + h + 1, :] = jnp.transpose(jnp.broadcast_to(log_norm, (rows, 128)))[0:1, :]
        grad_scores = (probs * (grad_probs - delta)).astype(BF16)
        dq_ref[:, cols] = (jnp.dot(grad_scores, keys, preferred_element_type=F32) * scale).astype(BF16)

    @pl.loop(1, n)
    def _(k):
        @pl.when(p.c - k >= 0)
        def _():
            across_stats(p.c - k).start()

    stats[p.c] = mine[...]

    @pl.loop(1, n)
    def _(k):
        @pl.when(p.c + k < n)
        def _():
            arrive(p.c + k).wait_recv()
            arrive_stats(p.c + k).wait_recv()

    key_at = p.c * rows + lax.broadcasted_iota(jnp.int32, (rows, seq), 0)
    query_at = lax.broadcasted_iota(jnp.int32, (rows, seq), 1)
    allowed = key_at <= query_at
    for h in range(heads):
        cols = pl.ds(h * HEAD_DIM, HEAD_DIM)
        queries = kvq_ref[:, :, 2 * width + h * HEAD_DIM:2 * width + (h + 1) * HEAD_DIM].reshape(
            seq, HEAD_DIM
        )
        upstream = g_all[:, :, h * HEAD_DIM:(h + 1) * HEAD_DIM].reshape(seq, HEAD_DIM)
        queries = jnp.where(late, queries, nothing)
        upstream = jnp.where(late, upstream, nothing)
        keys = kvq_ref[p.c, :, pl.ds(h * HEAD_DIM, HEAD_DIM)]
        values = kvq_ref[p.c, :, pl.ds(width + h * HEAD_DIM, HEAD_DIM)]
        delta = jnp.concatenate([stats[s, h:h + 1, :] for s in range(n)], axis=1)
        log_norm = jnp.concatenate([stats[s, heads + h:heads + h + 1, :] for s in range(n)], axis=1)
        scores = contract_last(keys, queries) * scale
        probs = jnp.where(allowed, jnp.exp(jnp.where(allowed, scores - log_norm, 0.0)), 0.0)
        grad_scores = jnp.where(
            allowed, probs * (contract_last(values, upstream) - delta), 0.0
        ).astype(BF16)
        dv_ref[:, cols] = jnp.dot(probs.astype(BF16), upstream, preferred_element_type=F32).astype(BF16)
        dk_ref[:, cols] = (jnp.dot(grad_scores, queries, preferred_element_type=F32) * scale).astype(BF16)

    @pl.loop(1, n)
    def _(k):
        @pl.when(p.c - k >= 0)
        def _():
            across(p.c - k).wait_send()
            across_stats(p.c - k).wait_send()


def params(collective_id, grid=False):
    return pltpu.CompilerParams(
        collective_id=collective_id,
        has_side_effects=True,
        vmem_limit_bytes=56 * 1024 * 1024,
        **({"dimension_semantics": ("arbitrary",)} if grid else {}),
    )


def plain_route(
    dims, sizes, send_rows, mixed_in, grad_out, dense_gate, dense_up, dense_down,
    expert_gate, expert_up, expert_down, kvq
):
    n, tp, ep = dims
    group = tp * ep
    capacity, pair, chunk = sizes
    rows, width = mixed_in.shape
    part = width // group
    sem = pltpu.SemaphoreType.DMA
    ff = dense_gate.shape[0]
    ff_tile = tile_of(ff, 320)
    weight_spec = pl.BlockSpec((ff_tile, width), lambda i: (i, 0))
    full = pl.BlockSpec((rows, width), lambda i: (0, 0))
    arrived, dense_part = pl.pallas_call(
        functools.partial(dispatch_kernel, dims, ff // ff_tile),
        grid=(ff // ff_tile,),
        out_shape=(
            jax.ShapeDtypeStruct((tp, ep, n, pair, part), BF16),
            jax.ShapeDtypeStruct((rows, width), BF16),
        ),
        in_specs=[ANY, full, full, weight_spec, weight_spec, weight_spec],
        out_specs=(ANY, full),
        scratch_shapes=[pltpu.VMEM((rows, width), F32)]
        + [sem((n,))] * 2 + [sem((ep, n))] * 4 + [sem],
        compiler_params=params(1, True),
        name="dispatch_dense",
    )(send_rows, mixed_in, grad_out, dense_gate, dense_up, dense_down)

    arrived = arrived.reshape(group, n, pair, part)

    def joined(low):
        return arrived[:, :, low:low + capacity].transpose(1, 2, 0, 3).reshape(n * capacity, width)

    head_width = kvq.shape[1] // 3
    eh = expert_gate.shape[1]
    eh_tile = tile_of(eh, 320)
    weight_spec = pl.BlockSpec((1, eh_tile, width), lambda i: (0, i, 0))
    full = pl.BlockSpec((n * capacity, width), lambda i: (0, 0))
    expert_part, kvq_all = pl.pallas_call(
        functools.partial(expert_kernel, dims, eh // eh_tile),
        grid=(eh // eh_tile,),
        out_shape=(
            jax.ShapeDtypeStruct((n * capacity, width), BF16),
            jax.ShapeDtypeStruct((n, rows, 3 * head_width), BF16),
        ),
        in_specs=[full, full, weight_spec, weight_spec, weight_spec, ANY],
        out_specs=(full, ANY),
        scratch_shapes=[pltpu.VMEM((n * capacity, width), F32)] + [sem((n,))] * 2 + [sem],
        compiler_params=params(2, True),
        name="expert_gather",
    )(joined(0), joined(capacity), expert_gate, expert_up, expert_down, kvq)

    dense_chunks = -(-rows // chunk)
    chunks = n + dense_chunks
    expert_part = jnp.pad(
        expert_part.reshape(n, capacity, group, part), ((0, 0), (0, chunk - capacity), (0, 0), (0, 0))
    )
    dense_part = jnp.pad(
        dense_part.reshape(rows, group, part), ((0, dense_chunks * chunk - rows), (0, 0), (0, 0))
    ).reshape(dense_chunks, chunk, group, part)
    parts = jnp.concatenate([expert_part, dense_part], axis=0).transpose(2, 0, 1, 3)
    parts = parts.reshape(tp, ep, chunks, chunk, part)
    returned, dense_sum = pl.pallas_call(
        functools.partial(return_kernel, dims, chunks),
        out_shape=(
            jax.ShapeDtypeStruct((n, chunk, part), BF16),
            jax.ShapeDtypeStruct((dense_chunks, chunk, part), F32),
        ),
        in_specs=[WHOLE],
        out_specs=(WHOLE, WHOLE),
        scratch_shapes=[
            pltpu.VMEM((ep, chunks, chunk, part), BF16),
            pltpu.VMEM((ep, chunks, chunk, part), BF16),
            pltpu.VMEM((ep, chunks, chunk, part), BF16),
            pltpu.VMEM((n, chunk, part), BF16),
        ]
        + [sem((ep, chunks))] * 4 + [sem((n,))] * 2,
        compiler_params=params(3),
        name="return_rows",
    )(parts)
    return returned, dense_sum, kvq_all


def fused_route(
    dims, sizes, send_rows, mixed_in, grad_out, dense_gate, dense_up, dense_down,
    expert_gate, expert_up, expert_down, kvq
):
    n, tp, ep = dims
    capacity, pair, chunk = sizes
    rows, width = mixed_in.shape
    part = width // (tp * ep)
    sem = pltpu.SemaphoreType.DMA
    eh = expert_gate.shape[1]
    dense_chunks = -(-rows // chunk)
    chunks = n + dense_chunks
    return pl.pallas_call(
        functools.partial(experts_kernel, dims, capacity),
        out_shape=(
            jax.ShapeDtypeStruct((n, chunk, part), BF16),
            jax.ShapeDtypeStruct((dense_chunks, chunk, part), F32),
            jax.ShapeDtypeStruct((n,) + kvq.shape, BF16),
        ),
        in_specs=[ANY, WHOLE, WHOLE] + [ANY] * 7,
        out_specs=(WHOLE, WHOLE, ANY),
        scratch_shapes=[
            pltpu.VMEM((n, pair, width), BF16),
            pltpu.VMEM((n * capacity, width), BF16),
            pltpu.VMEM((n * capacity, width), BF16),
            pltpu.VMEM((3, max(eh, dense_gate.shape[0]), width), BF16),
            pltpu.VMEM((n * capacity, eh), BF16),
            pltpu.VMEM((n * capacity, eh), BF16),
            pltpu.VMEM((chunks, chunk, width), BF16),
            pltpu.VMEM((ep, chunks, chunk, part), BF16),
            pltpu.VMEM((max(ep - 1, 1), chunks, chunk, part), BF16),
            pltpu.VMEM((max(ep - 1, 1), chunks, chunk, part), BF16),
            pltpu.VMEM((n, chunk, part), BF16),
        ]
        + [sem((n,))] * 2 + [sem((ep, n))] * 4 + [sem((ep, chunks))] * 4 + [sem((n,))] * 6
        + [sem((3,)), sem((2,))],
        compiler_params=params(6),
        name="experts",
    )(
        send_rows, mixed_in, grad_out, dense_gate, dense_up, dense_down,
        expert_gate, expert_up, expert_down, kvq
    )


def body(
    dims, hidden, grad_out, gain, dense_gate, dense_up, dense_down, expert_gate, expert_up, expert_down,
    out_proj, queries, keys, values, route_ids, route_weights
):
    n, tp, ep = dims
    group = tp * ep
    rows, width = hidden.shape
    part = width // group
    picks = route_ids.shape[1]
    capacity = 5 * rows // (2 * n)
    pair = round_up(2 * capacity, 16)
    chunk = round_up(capacity, 16)
    sem = pltpu.SemaphoreType.DMA
    at = lax.axis_index("tp") * ep + lax.axis_index("ep")

    hidden_f = hidden.astype(F32)
    inverse = lax.rsqrt(jnp.mean(hidden_f * hidden_f, axis=1, keepdims=True) + EPSILON)
    normed = hidden_f * inverse
    mixed_in = (normed * gain).astype(BF16)

    flat_ids = route_ids.reshape(-1)
    hits = (flat_ids[:, None] == lax.iota(jnp.int32, n)[None, :]).astype(BF16)
    order = lax.iota(jnp.int32, picks * rows)
    before = (order[None, :] < order[:, None]).astype(BF16)
    earlier = jnp.dot(before, hits, preferred_element_type=F32)
    slots = jnp.sum(earlier * hits.astype(F32), axis=1).astype(jnp.int32)
    slots = slots.reshape(rows, picks)
    pair_at = (route_ids * pair + slots).T
    home_at = route_ids * chunk + slots
    places = lax.iota(jnp.int32, n * pair)[:, None]
    own_in = lax.dynamic_slice(mixed_in, (0, at * part), (rows, part))
    own_out = lax.dynamic_slice(grad_out, (0, at * part), (rows, part))
    pick_in = sum((places == pair_at[k][None, :]).astype(BF16) for k in range(picks))
    pick_out = [(places == pair_at[k][None, :] + capacity) for k in range(picks)]
    weight_of = sum(
        jnp.sum(jnp.where(pick_out[k], route_weights[:, k][None, :], 0.0), axis=1, keepdims=True)
        for k in range(picks)
    )
    pick_out = sum(hit.astype(BF16) for hit in pick_out)
    send_rows = (
        jnp.dot(pick_in, own_in, preferred_element_type=F32)
        + jnp.dot(pick_out, own_out, preferred_element_type=F32) * weight_of
    ).astype(BF16).reshape(n, pair, part)

    kvq = jnp.concatenate([keys, values, queries], axis=1)
    head_width = queries.shape[1]
    route = fused_route if part % 128 == 0 else plain_route
    returned, dense_sum, kvq_all = route(
        dims, (capacity, pair, chunk), send_rows, mixed_in, grad_out, dense_gate, dense_up, dense_down,
        expert_gate, expert_up, expert_down, kvq
    )

    home_places = lax.iota(jnp.int32, n * chunk)[None, :]
    take = sum((home_places == home_at[:, k:k + 1]).astype(BF16) for k in range(picks))
    own_total = (
        jnp.dot(take, returned.reshape(n * chunk, part), preferred_element_type=F32)
        + dense_sum.reshape(-1, part)[:rows]
    ).astype(BF16)
    total_grad = pl.pallas_call(
        functools.partial(group_kernel, dims),
        out_shape=jax.ShapeDtypeStruct((tp, ep, rows, part), BF16),
        in_specs=[WHOLE],
        out_specs=WHOLE,
        scratch_shapes=[sem((ep,))] * 4,
        compiler_params=params(4),
        name="group_gather",
    )(own_total)
    total_grad = total_grad.reshape(group, rows, part).transpose(1, 0, 2).reshape(rows, width).astype(F32)
    scaled_grad = total_grad * gain
    grad_hidden = (
        grad_out.astype(F32)
        + inverse * (scaled_grad - normed * jnp.mean(scaled_grad * normed, axis=1, keepdims=True))
    ).astype(BF16)
    grad_heads = contract_last(grad_hidden, out_proj).astype(BF16)

    heads = head_width // HEAD_DIM
    stat_rows = round_up(2 * heads, 8)
    grads = jax.ShapeDtypeStruct((rows, head_width), BF16)
    grad_queries, grad_keys, grad_values = pl.pallas_call(
        functools.partial(attention_kernel, dims),
        out_shape=(grads, grads, grads),
        in_specs=[WHOLE, WHOLE],
        out_specs=(WHOLE, WHOLE, WHOLE),
        scratch_shapes=[
            pltpu.VMEM((n, rows, head_width), BF16),
            pltpu.VMEM((n, stat_rows, rows), F32),
            pltpu.VMEM((stat_rows, rows), F32),
        ]
        + [sem((n,))] * 4,
        compiler_params=params(5),
        name="attention_grads",
    )(grad_heads, kvq_all)
    return (grad_hidden, grad_queries, grad_keys, grad_values)


def solution(mesh):
    dims = (mesh.shape["ctx"], mesh.shape["tp"], mesh.shape["ep"])
    hidden_units = P(("tp", "ep"), None)
    expert_units = P("ctx", ("tp", "ep"), None)
    by_head = P("ctx", ("tp", "ep"))
    return jax.shard_map(
        functools.partial(body, dims),
        mesh=mesh,
        in_specs=(
            P("ctx", None), P("ctx", None), P(),
            hidden_units, hidden_units, hidden_units,
            expert_units, expert_units, expert_units,
            hidden_units, by_head, by_head, by_head,
            P("ctx", None), P("ctx", None),
        ),
        out_specs=(P("ctx", None), by_head, by_head, by_head),
        check_vma=False,
    )
```

```python
import functools

import jax
import jax.numpy as jnp
from jax import lax
from jax.experimental import pallas as pl
from jax.experimental.pallas import tpu as pltpu
from jax.sharding import PartitionSpec as P

HEAD_DIM = 128
NEG_FILL = -1e30
EPSILON = 1e-05
MESH = pl.DeviceIdType.MESH
ANY = pl.BlockSpec(memory_space=pl.ANY)
WHOLE = pl.BlockSpec(memory_space=pltpu.VMEM)
BF16 = jnp.bfloat16
F32 = jnp.float32


def contract_last(left_rows, right_rows):
    return lax.dot_general(
        left_rows, right_rows, (((1,), (1,)), ((), ())), preferred_element_type=F32
    )


def round_up(value, step):
    return -(-value // step) * step


def tile_of(hidden, most):
    fits = [t for t in range(16, most + 1, 16) if hidden % t == 0]
    return max(fits) if fits else hidden


class Place:
    def __init__(self, n, tp, ep):
        self.n, self.tp, self.ep = n, tp, ep
        self.c = lax.axis_index("ctx")
        self.t = lax.axis_index("tp")
        self.e = lax.axis_index("ep")

    def ctx_peer(self, k):
        return lax.rem(self.c + k, self.n)

    def ctx_from(self, k):
        return lax.rem(self.c + self.n - k, self.n)

    def ep_peer(self, b):
        return lax.rem(self.e + b, self.ep)

    def ep_from(self, b):
        return lax.rem(self.e + self.ep - b, self.ep)

    def at(self, c=None, t=None, e=None):
        return (
            self.c if c is None else c,
            self.t if t is None else t,
            self.e if e is None else e,
        )

    def greet(self, ctx, group):
        barrier = pltpu.get_barrier_semaphore()
        total = 0
        if ctx:
            for k in range(1, self.n):
                pl.semaphore_signal(
                    barrier, 1, device_id=self.at(c=self.ctx_peer(k)), device_id_type=MESH
                )
            total += self.n - 1
        if group:
            for b in range(1, self.ep):
                pl.semaphore_signal(
                    barrier, 1, device_id=self.at(e=self.ep_peer(b)), device_id_type=MESH
                )
            pl.semaphore_signal(barrier, 1, device_id=self.at(t=1 - self.t), device_id_type=MESH)
            total += self.ep
        pl.semaphore_wait(barrier, total)


def remote(src, dst, send, recv, device):
    return pltpu.make_async_remote_copy(
        src_ref=src, dst_ref=dst, send_sem=send, recv_sem=recv, device_id=device, device_id_type=MESH
    )


def swiglu_tile(x_ref, y_ref, gate_ref, up_ref, down_ref, acc_ref, first):
    a = contract_last(x_ref[...], gate_ref[...])
    b = contract_last(x_ref[...], up_ref[...])
    back = contract_last(y_ref[...], down_ref[...])
    s = jax.nn.sigmoid(a)
    grad_a = (back * b * s * (1.0 + a * (1.0 - s))).astype(BF16)
    grad_b = (back * a * s).astype(BF16)
    width = acc_ref.shape[1]
    step = 512 if width % 512 == 0 else width
    for at in range(0, width, step):
        cols = pl.ds(at, step)
        term = jnp.dot(grad_a, gate_ref[:, cols], preferred_element_type=F32) + jnp.dot(
            grad_b, up_ref[:, cols], preferred_element_type=F32
        )

        @pl.when(first)
        def _():
            acc_ref[:, cols] = term

        @pl.when(jnp.logical_not(first))
        def _():
            acc_ref[:, cols] = acc_ref[:, cols] + term


def dispatch_kernel(
    dims, tiles, rows_ref, x_ref, y_ref, gate_ref, up_ref, down_ref,
    out_ref, part_ref, acc_ref, send1, recv1, send2, recv2, send3, recv3, local
):
    p = Place(*dims)
    step = pl.program_id(0)

    def across(k):
        d = p.ctx_peer(k)
        return remote(rows_ref.at[d], out_ref.at[p.t, p.e, p.c], send1.at[d], recv1.at[p.c], p.at(c=d))

    def arrive(src):
        return remote(
            rows_ref.at[src], out_ref.at[p.t, p.e, src], send1.at[src], recv1.at[src], p.at(c=src)
        )

    def to_ep(b, src, own):
        block = rows_ref.at[src] if own else out_ref.at[p.t, p.e, src]
        return remote(
            block, out_ref.at[p.t, p.e, src], send2.at[b, src], recv2.at[b, src], p.at(e=p.ep_peer(b))
        )

    def from_ep(b, src):
        e = p.ep_from(b)
        return remote(
            out_ref.at[p.t, e, src], out_ref.at[p.t, e, src], send2.at[b, src], recv2.at[b, src], p.at(e=e)
        )

    def to_core(e, src, own=False):
        block = rows_ref.at[src] if own else out_ref.at[p.t, e, src]
        return remote(
            block, out_ref.at[p.t, e, src], send3.at[e, src], recv3.at[e, src], p.at(t=1 - p.t)
        )

    def from_core(e, src):
        block = out_ref.at[1 - p.t, e, src]
        return remote(block, block, send3.at[e, src], recv3.at[e, src], p.at(t=1 - p.t))

    def keep():
        return pltpu.make_async_copy(rows_ref.at[p.c], out_ref.at[p.t, p.e, p.c], local)

    @pl.when(step == 0)
    def _():
        p.greet(True, True)

        @pl.loop(1, p.n)
        def _(k):
            across(k).start()

        for b in range(1, p.ep):
            to_ep(b, p.c, True).start()
        to_core(p.e, p.c, True).start()
        keep().start()

    swiglu_tile(x_ref, y_ref, gate_ref, up_ref, down_ref, acc_ref, step == 0)

    @pl.when(step == tiles - 1)
    def _():
        part_ref[...] = acc_ref[...].astype(BF16)

        def pass_on(src):
            for b in range(1, p.ep):
                from_ep(b, src).wait_recv()
                to_core(p.ep_from(b), src).start()

        @pl.loop(1, p.n)
        def _(k):
            src = p.ctx_from(k)
            arrive(src).wait_recv()
            for b in range(1, p.ep):
                to_ep(b, src, False).start()
            to_core(p.e, src).start()
            pass_on(p.ctx_from(k - 1))

        pass_on(p.ctx_from(p.n - 1))
        keep().wait()

        @pl.loop(0, p.n)
        def _(src):
            for e in range(p.ep):
                from_core(e, src).wait_recv()
                to_core(e, src).wait_send()
            for b in range(1, p.ep):
                to_ep(b, src, False).wait_send()

        @pl.loop(1, p.n)
        def _(k):
            across(k).wait_send()


def expert_kernel(
    dims, tiles, x_ref, y_ref, gate_ref, up_ref, down_ref, kvq_ref,
    out_ref, all_ref, acc_ref, send, recv, local
):
    p = Place(*dims)
    step = pl.program_id(0)

    def across(k):
        d = p.ctx_peer(k)
        return remote(kvq_ref, all_ref.at[p.c], send.at[d], recv.at[p.c], p.at(c=d))

    def arrive(src):
        return remote(kvq_ref, all_ref.at[src], send.at[src], recv.at[src], p.at(c=src))

    def keep():
        return pltpu.make_async_copy(kvq_ref, all_ref.at[p.c], local)

    @pl.when(step == 0)
    def _():
        p.greet(True, False)

        @pl.loop(1, p.n)
        def _(k):
            across(k).start()

        keep().start()

    swiglu_tile(x_ref, y_ref, gate_ref.at[0], up_ref.at[0], down_ref.at[0], acc_ref, step == 0)

    @pl.when(step == tiles - 1)
    def _():
        out_ref[...] = acc_ref[...].astype(BF16)
        keep().wait()

        @pl.loop(1, p.n)
        def _(k):
            arrive(p.ctx_from(k)).wait_recv()
            across(k).wait_send()


def return_kernel(
    dims, chunks, part_ref, back_ref, dense_ref,
    core_buf, ep_out, ep_in, fin_ref, send1, recv1, send2, recv2, send3, recv3
):
    p = Place(*dims)
    p.greet(True, True)

    def to_core(e, i):
        return remote(
            part_ref.at[1 - p.t, e, i], core_buf.at[e, i], send1.at[e, i], recv1.at[e, i], p.at(t=1 - p.t)
        )

    def to_ep(b, i):
        return remote(
            ep_out.at[b, i], ep_in.at[b, i], send2.at[b, i], recv2.at[b, i], p.at(e=p.ep_peer(b))
        )

    def home(d):
        return remote(fin_ref.at[d], back_ref.at[p.c], send3.at[d], recv3.at[p.c], p.at(c=d))

    def arrive(src):
        return remote(fin_ref.at[src], back_ref.at[src], send3.at[src], recv3.at[src], p.at(c=src))

    def chunk_of(k):
        return jnp.where(k < p.n, lax.rem(p.c + k + 1, p.n), k)

    @pl.loop(0, chunks)
    def _(k):
        i = chunk_of(k)
        for b in range(1, p.ep):
            to_core(p.ep_peer(b), i).start()
        to_core(p.e, i).start()

    @pl.loop(0, chunks)
    def _(k):
        i = chunk_of(k)
        for b in range(1, p.ep):
            e = p.ep_peer(b)
            to_core(e, i).wait_recv()
            ep_out[b, i] = (part_ref[p.t, e, i].astype(F32) + core_buf[e, i].astype(F32)).astype(BF16)
            to_ep(b, i).start()

    def total(i):
        to_core(p.e, i).wait_recv()
        value = part_ref[p.t, p.e, i].astype(F32) + core_buf[p.e, i].astype(F32)
        for b in range(1, p.ep):
            to_ep(b, i).wait_recv()
            value = value + ep_in[b, i].astype(F32)
        return value

    @pl.loop(0, p.n - 1)
    def _(k):
        i = chunk_of(k)
        fin_ref[i] = total(i).astype(BF16)
        home(i).start()

    back_ref[p.c] = total(p.c).astype(BF16)

    @pl.loop(p.n, chunks)
    def _(i):
        dense_ref[i - p.n] = total(i)

    @pl.loop(1, p.n)
    def _(k):
        arrive(p.ctx_from(k)).wait_recv()
        home(p.ctx_peer(k)).wait_send()

    @pl.loop(0, chunks)
    def _(i):
        for b in range(1, p.ep):
            to_ep(b, i).wait_send()
        for e in range(p.ep):
            to_core(e, i).wait_send()


def experts_kernel(
    dims, capacity, rows_ref, x_ref, y_ref, hidden_ref, gain_ref, home_ref, proj_ref,
    k_ref, v_ref, q_ref, dense_gate, dense_up, dense_down, expert_gate, expert_up, expert_down,
    hidden_out, heads_out,
    got, x_in, y_in, weights, grad_a, grad_b, out, core_buf, ep_out, ep_in, fin_ref, back_ref,
    dense_ref, joint, k_all, v_all, q_all, g_all, probs_ref, turned_ref, norms, deltas, my_norms, my_deltas,
    send1, recv1, send2, recv2, send3, recv3, send4, recv4, send5, recv5, send6, recv6,
    send7, recv7, send8, recv8, sent, landed, loads, local
):
    p = Place(*dims)
    n = p.n
    part = rows_ref.shape[2]
    rows, width = x_ref.shape
    ff, eh = dense_gate.shape[0], expert_gate.shape[1]
    chunks, chunk = out.shape[0], out.shape[1]
    head_width = k_ref.shape[1]
    heads = head_width // HEAD_DIM
    seq = n * rows
    scale = HEAD_DIM ** (-0.5)

    def cols(t, e):
        return pl.ds(pl.multiple_of((t * p.ep + e) * part, 128), part)

    def across(k):
        d = p.ctx_peer(k)
        return remote(
            rows_ref.at[d], got.at[p.c, :, cols(p.t, p.e)], send1.at[d], recv1.at[p.c], p.at(c=d)
        )

    def arrive(src):
        return remote(
            rows_ref.at[src], got.at[src, :, cols(p.t, p.e)], send1.at[src], recv1.at[src], p.at(c=src)
        )

    def to_ep(b, src, own=False):
        slot = got.at[src, :, cols(p.t, p.e)]
        return remote(
            rows_ref.at[src] if own else slot, slot, send2.at[b, src], recv2.at[b, src],
            p.at(e=p.ep_peer(b)),
        )

    def from_ep(b, src):
        e = p.ep_from(b)
        slot = got.at[src, :, cols(p.t, e)]
        return remote(slot, slot, send2.at[b, src], recv2.at[b, src], p.at(e=e))

    def to_core(e, src, own=False):
        slot = got.at[src, :, cols(p.t, e)]
        return remote(
            rows_ref.at[src] if own else slot, slot, send3.at[e, src], recv3.at[e, src], p.at(t=1 - p.t)
        )

    def from_core(e, src):
        slot = got.at[src, :, cols(1 - p.t, e)]
        return remote(slot, slot, send3.at[e, src], recv3.at[e, src], p.at(t=1 - p.t))

    def keep():
        return pltpu.make_async_copy(rows_ref.at[p.c], got.at[p.c, :, cols(p.t, p.e)], local.at[0])

    def pass_on(src):
        for b in range(1, p.ep):
            from_ep(b, src).wait_recv()
            to_core(p.ep_from(b), src).start()

    def forward(at):
        src = p.ctx_from(shifts[at])
        arrive(src).wait_recv()
        if at + 3 < n - 1:
            across(shifts[at + 3]).start()
        for b in range(1, p.ep):
            to_ep(b, src).start()
        to_core(p.e, src).start()
        pass_on(p.ctx_from(shifts[at - 1] if at else 0))

    def sum_core(e, i):
        return remote(
            out.at[i, :, cols(1 - p.t, e)], core_buf.at[e, i], send4.at[e, i], recv4.at[e, i],
            p.at(t=1 - p.t),
        )

    def sum_ep(b, i):
        return remote(
            ep_out.at[b - 1, i], ep_in.at[b - 1, i], send5.at[b, i], recv5.at[b, i], p.at(e=p.ep_peer(b))
        )

    def pass_sum(b, i):
        e = p.ep_peer(b)
        sum_core(e, i).wait_recv()
        ep_out[b - 1, i] = (out[i, :, cols(p.t, e)].astype(F32) + core_buf[e, i].astype(F32)).astype(BF16)
        sum_ep(b, i).start()

    def total(i):
        sum_core(p.e, i).wait_recv()
        value = out[i, :, cols(p.t, p.e)].astype(F32) + core_buf[p.e, i].astype(F32)
        for b in range(1, p.ep):
            sum_ep(b, i).wait_recv()
            value = value + ep_in[b - 1, i].astype(F32)
        return value

    def home(d):
        return remote(fin_ref.at[d], back_ref.at[p.c], send6.at[d], recv6.at[p.c], p.at(c=d))

    def home_from(src):
        return remote(fin_ref.at[src], back_ref.at[src], send6.at[src], recv6.at[src], p.at(c=src))

    shared = [
        (k_ref, k_all, 1), (v_ref, v_all, 1), (q_ref, q_all, -1),
        (my_norms, norms, -1), (g_all.at[p.c], g_all, -1), (my_deltas, deltas, -1),
    ]

    def share(j, d):
        src, dst, _ = shared[j]
        return remote(src, dst.at[p.c], sent.at[j, d], landed.at[j, p.c], p.at(c=d))

    def shared_from(j, src):
        block, dst, _ = shared[j]
        return remote(block, dst.at[src], sent.at[j, src], landed.at[j, src], p.at(c=src))

    def each(items, onward, act):
        @pl.loop(1, n)
        def _(k):
            for j in items:
                up = (shared[j][2] > 0) == onward
                peer = p.c + k if up else p.c - k

                @pl.when(peer < n if up else peer >= 0)
                def _():
                    act(j, peer)

    def share_all(*items):
        each(items, True, lambda j, d: share(j, d).start())

    def wait_all(*items):
        each(items, False, lambda j, src: shared_from(j, src).wait_recv())

    def joint_ep(b, mine):
        e = p.e if mine else p.ep_from(b)
        slot = joint.at[:, cols(p.t, e)]
        return remote(slot, slot, send7.at[b], recv7.at[b], p.at(e=p.ep_peer(b)))

    def joint_core(e, mine):
        slot = joint.at[:, cols(p.t if mine else 1 - p.t, e)]
        return remote(slot, slot, send8.at[e], recv8.at[e], p.at(t=1 - p.t))

    def load(j, ref, size):
        return pltpu.make_async_copy(ref, weights.at[j, pl.ds(0, size)], loads.at[j])

    dense = [load(j, ref, ff) for j, ref in enumerate((dense_gate, dense_up, dense_down))]
    expert = [
        load(j, ref.at[0], eh) for j, ref in enumerate((expert_gate, expert_up, expert_down))
    ]
    for copy in dense:
        copy.start()
    for ref in (k_all, v_all, q_all, g_all, norms, deltas, my_norms, my_deltas):
        ref[...] = jnp.zeros_like(ref)
    p.greet(True, True)
    shifts = sorted(range(1, n), key=lambda k: abs(2 * k - n))

    for k in shifts[:3]:
        across(k).start()
    for b in range(1, p.ep):
        to_ep(b, p.c, True).start()
    to_core(p.e, p.c, True).start()
    keep().start()
    k_all[p.c] = k_ref[...]
    v_all[p.c] = v_ref[...]
    q_all[p.c] = q_ref[...]

    def slopes(a, b, back):
        s = jax.nn.sigmoid(a)
        return (back * b * s * (1.0 + a * (1.0 - s))).astype(BF16), (back * a * s).astype(BF16)

    for copy in dense:
        copy.wait()
    da, db = slopes(
        contract_last(x_ref[...], weights[0, 0:ff, :]),
        contract_last(x_ref[...], weights[1, 0:ff, :]),
        contract_last(y_ref[...], weights[2, 0:ff, :]),
    )
    step = 512 if width % 512 == 0 else width
    done = 0
    for low in range(0, width, step):
        if low * 2 >= width * done and done < min(2, n - 1):
            forward(done)
            done += 1
        term = jnp.dot(da, weights[0, 0:ff, low:low + step], preferred_element_type=F32) + jnp.dot(
            db, weights[1, 0:ff, low:low + step], preferred_element_type=F32
        )
        for j in range(chunks - n):
            piece = term[j * chunk:min((j + 1) * chunk, rows)]
            if piece.shape[0] < chunk:
                piece = jnp.concatenate(
                    [piece, jnp.zeros((chunk - piece.shape[0], step), F32)], axis=0
                )
            out[n + j, :, low:low + step] = piece.astype(BF16)
    for copy in expert:
        copy.start()

    @pl.loop(n, chunks)
    def _(i):
        for e in range(p.ep):
            sum_core(e, i).start()

    for at in range(done, n - 1):
        forward(at)
    pass_on(p.ctx_from(shifts[-1]))
    keep().wait()

    share_all(0, 1, 2)
    for k in range(n):
        src = p.ctx_from(k)
        for e in range(p.ep):
            from_core(e, src).wait_recv()
        x_in[k * capacity:(k + 1) * capacity, :] = got[src, 0:capacity, :]
        y_in[k * capacity:(k + 1) * capacity, :] = got[src, capacity:2 * capacity, :]

    for copy in expert:
        copy.wait()
    for low in range(0, eh, 256):
        high = min(low + 256, eh)
        ga, gb = slopes(
            contract_last(x_in[...], weights[0, low:high, :]),
            contract_last(x_in[...], weights[1, low:high, :]),
            contract_last(y_in[...], weights[2, low:high, :]),
        )
        grad_a[:, low:high] = ga
        grad_b[:, low:high] = gb
        if low == 0:

            @pl.loop(n, chunks)
            def _(i):
                for b in range(1, p.ep):
                    pass_sum(b, i)

    def chunk_of(k):
        return lax.rem(p.c + k + 1, n)

    for mine in (False, True):
        for b in list(range(1, p.ep)) + [0]:
            t, e = (p.t if mine else 1 - p.t), p.ep_peer(b)
            value = jnp.dot(grad_a[...], weights[0, 0:eh, cols(t, e)], preferred_element_type=F32) + jnp.dot(
                grad_b[...], weights[1, 0:eh, cols(t, e)], preferred_element_type=F32
            )
            for k in range(n):
                piece = jnp.concatenate(
                    [value[k * capacity:(k + 1) * capacity], jnp.zeros((chunk - capacity, part), F32)],
                    axis=0,
                )
                out[p.ctx_from(k), :, cols(t, e)] = piece.astype(BF16)
            if not mine:

                @pl.loop(0, n)
                def _(k):
                    sum_core(e, chunk_of(k)).start()

            elif b:

                @pl.loop(0, n)
                def _(k):
                    pass_sum(b, chunk_of(k))

    @pl.loop(0, n - 1)
    def _(k):
        i = chunk_of(k)
        fin_ref[i] = total(i).astype(BF16)
        home(i).start()

    back_ref[p.c] = total(p.c).astype(BF16)

    for i in range(n, chunks):
        dense_ref[(i - n) * chunk:(i - n + 1) * chunk, :] = total(i)

    wait_all(0, 1)
    query_at = p.c * rows + lax.broadcasted_iota(jnp.int32, (rows, seq), 0)
    key_at = lax.broadcasted_iota(jnp.int32, (rows, seq), 1)
    allowed = key_at <= query_at
    heads_at = [slice(h * HEAD_DIM, (h + 1) * HEAD_DIM) for h in range(heads)]

    def across_rows(column):
        return jnp.transpose(jnp.broadcast_to(column, (rows, 128)))[0:1, :]

    for h, at in enumerate(heads_at):
        keys = k_all[:, :, at].reshape(seq, HEAD_DIM)
        scores = jnp.where(allowed, contract_last(q_ref[:, at], keys) * scale, NEG_FILL)
        top = jnp.max(scores, axis=1, keepdims=True)
        powers = jnp.where(allowed, jnp.exp(scores - top), 0.0)
        norm = jnp.sum(powers, axis=1, keepdims=True)
        probs_ref[h] = powers / norm
        my_norms[h:h + 1, :] = across_rows(top + jnp.log(norm))
    share_all(3)
    norms[p.c] = my_norms[...]

    @pl.loop(1, n)
    def _(k):
        home_from(p.ctx_from(k)).wait_recv()

    spots = lax.broadcasted_iota(jnp.int32, (rows, n * chunk), 1)
    take = sum(
        jnp.where(spots == home_ref[:, k:k + 1], 1.0, 0.0) for k in range(home_ref.shape[1])
    ).astype(BF16)
    joint[:, cols(p.t, p.e)] = (
        jnp.dot(take, back_ref[...].reshape(n * chunk, part), preferred_element_type=F32)
        + dense_ref[0:rows, :]
    ).astype(BF16)
    for b in range(1, p.ep):
        joint_ep(b, True).start()
    joint_core(p.e, True).start()

    wait_all(2, 3)
    turned_key = p.c * rows + lax.broadcasted_iota(jnp.int32, (rows, seq), 0)
    turned_query = lax.broadcasted_iota(jnp.int32, (rows, seq), 1)
    turned_allowed = turned_key <= turned_query
    for h, at in enumerate(heads_at):
        queries = q_all[:, :, at].reshape(seq, HEAD_DIM)
        norm = jnp.concatenate([norms[s, h:h + 1, :] for s in range(n)], axis=1)
        scores = contract_last(k_ref[:, at], queries) * scale
        turned_ref[h] = jnp.where(
            turned_allowed, jnp.exp(jnp.where(turned_allowed, scores - norm, 0.0)), 0.0
        )

    for b in range(1, p.ep):
        joint_ep(b, False).wait_recv()
        joint_core(p.ep_from(b), True).start()
    hidden = hidden_ref[...].astype(F32)
    inverse = lax.rsqrt(jnp.mean(hidden * hidden, axis=1, keepdims=True) + EPSILON)
    for e in range(p.ep):
        joint_core(e, False).wait_recv()
    normed = hidden_ref[...].astype(F32) * inverse
    scaled = joint[...].astype(F32) * gain_ref[...]
    mean = jnp.mean(scaled * normed, axis=1, keepdims=True)
    hidden_out[...] = (y_ref[...].astype(F32) + inverse * (scaled - normed * mean)).astype(BF16)
    g_all[p.c] = contract_last(hidden_out[...], proj_ref[...]).astype(BF16)
    share_all(4)

    def grads(j, at, value):
        heads_out[j, :, at] = value.astype(BF16)

    g_own = g_all[p.c]
    spread = []
    for h, at in enumerate(heads_at):
        values = v_all[:, :, at].reshape(seq, HEAD_DIM)
        grad_probs = contract_last(g_own[:, at], values)
        delta = jnp.sum(probs_ref[h] * grad_probs, axis=1, keepdims=True)
        my_deltas[h:h + 1, :] = across_rows(delta)
        spread.append((probs_ref[h] * (grad_probs - delta)).astype(BF16))
    share_all(5)
    deltas[p.c] = my_deltas[...]
    for h, at in enumerate(heads_at):
        keys = k_all[:, :, at].reshape(seq, HEAD_DIM)
        grads(0, at, jnp.dot(spread[h], keys, preferred_element_type=F32) * scale)

    wait_all(4, 5)
    for h, at in enumerate(heads_at):
        queries = q_all[:, :, at].reshape(seq, HEAD_DIM)
        upstream = g_all[:, :, at].reshape(seq, HEAD_DIM)
        delta = jnp.concatenate([deltas[s, h:h + 1, :] for s in range(n)], axis=1)
        probs = turned_ref[h]
        grad_scores = (probs * (contract_last(v_ref[:, at], upstream) - delta)).astype(BF16)
        grads(1, at, jnp.dot(grad_scores, queries, preferred_element_type=F32) * scale)
        grads(2, at, jnp.dot(probs.astype(BF16), upstream, preferred_element_type=F32))

    each(range(len(shared)), True, lambda j, d: share(j, d).wait_send())
    for b in range(1, p.ep):
        joint_ep(b, True).wait_send()
    for e in range(p.ep):
        joint_core(e, True).wait_send()

    @pl.loop(1, n)
    def _(k):
        across(k).wait_send()
        home(p.ctx_peer(k)).wait_send()

    @pl.loop(0, n)
    def _(src):
        for e in range(p.ep):
            to_core(e, src).wait_send()
        for b in range(1, p.ep):
            to_ep(b, src).wait_send()

    @pl.loop(0, chunks)
    def _(i):
        for e in range(p.ep):
            sum_core(e, i).wait_send()
        for b in range(1, p.ep):
            sum_ep(b, i).wait_send()


def group_kernel(dims, own_ref, all_ref, send2, recv2, send3, recv3):
    p = Place(*dims)
    p.greet(False, True)
    all_ref[p.t, p.e] = own_ref[...]

    def to_ep(b):
        return remote(own_ref, all_ref.at[p.t, p.e], send2.at[b], recv2.at[b], p.at(e=p.ep_peer(b)))

    def from_ep(b):
        e = p.ep_from(b)
        return remote(own_ref, all_ref.at[p.t, e], send2.at[b], recv2.at[b], p.at(e=e))

    def to_core(e, own=False):
        block = own_ref if own else all_ref.at[p.t, e]
        return remote(block, all_ref.at[p.t, e], send3.at[e], recv3.at[e], p.at(t=1 - p.t))

    def from_core(e):
        block = all_ref.at[1 - p.t, e]
        return remote(block, block, send3.at[e], recv3.at[e], p.at(t=1 - p.t))

    for b in range(1, p.ep):
        to_ep(b).start()
    to_core(p.e, True).start()
    for b in range(1, p.ep):
        from_ep(b).wait_recv()
        to_core(p.ep_from(b)).start()
    for e in range(p.ep):
        from_core(e).wait_recv()
        to_core(e).wait_send()
    for b in range(1, p.ep):
        to_ep(b).wait_send()


def attention_kernel(
    dims, g_ref, kvq_ref, dq_ref, dk_ref, dv_ref, g_all, stats, mine, send1, recv1, send2, recv2
):
    p = Place(*dims)
    p.greet(True, False)
    n = p.n
    rows, width = g_ref.shape
    heads = width // HEAD_DIM
    seq = n * rows
    scale = HEAD_DIM ** (-0.5)

    def across(d):
        return remote(g_ref, g_all.at[p.c], send1.at[d], recv1.at[p.c], p.at(c=d))

    def across_stats(d):
        return remote(mine, stats.at[p.c], send2.at[d], recv2.at[p.c], p.at(c=d))

    def arrive(src):
        return remote(g_ref, g_all.at[src], send1.at[src], recv1.at[src], p.at(c=src))

    def arrive_stats(src):
        return remote(mine, stats.at[src], send2.at[src], recv2.at[src], p.at(c=src))

    @pl.loop(1, n)
    def _(k):
        @pl.when(p.c - k >= 0)
        def _():
            across(p.c - k).start()

    g_all[p.c] = g_ref[...]
    mine[...] = jnp.zeros_like(mine)
    token = lax.broadcasted_iota(jnp.int32, (seq, HEAD_DIM), 0)
    early = token < (p.c + 1) * rows
    late = token >= p.c * rows
    nothing = jnp.zeros((seq, HEAD_DIM), BF16)
    query_at = p.c * rows + lax.broadcasted_iota(jnp.int32, (rows, seq), 0)
    key_at = lax.broadcasted_iota(jnp.int32, (rows, seq), 1)
    allowed = key_at <= query_at
    for h in range(heads):
        cols = pl.ds(h * HEAD_DIM, HEAD_DIM)
        keys = kvq_ref[:, :, h * HEAD_DIM:(h + 1) * HEAD_DIM].reshape(seq, HEAD_DIM)
        values = kvq_ref[:, :, width + h * HEAD_DIM:width + (h + 1) * HEAD_DIM].reshape(seq, HEAD_DIM)
        keys = jnp.where(early, keys, nothing)
        values = jnp.where(early, values, nothing)
        q = kvq_ref[p.c, :, pl.ds(2 * width + h * HEAD_DIM, HEAD_DIM)]
        scores = jnp.where(allowed, contract_last(q, keys) * scale, NEG_FILL)
        top = jnp.max(scores, axis=1, keepdims=True)
        weights = jnp.where(allowed, jnp.exp(scores - top), 0.0)
        total = jnp.sum(weights, axis=1, keepdims=True)
        probs = weights / total
        grad_probs = contract_last(g_ref[:, cols], values)
        delta = jnp.sum(probs * grad_probs, axis=1, keepdims=True)
        log_norm = top + jnp.log(total)
        mine[h:h + 1, :] = jnp.transpose(jnp.broadcast_to(delta, (rows, 128)))[0:1, :]
        mine[heads + h:heads + h + 1, :] = jnp.transpose(jnp.broadcast_to(log_norm, (rows, 128)))[0:1, :]
        grad_scores = (probs * (grad_probs - delta)).astype(BF16)
        dq_ref[:, cols] = (jnp.dot(grad_scores, keys, preferred_element_type=F32) * scale).astype(BF16)

    @pl.loop(1, n)
    def _(k):
        @pl.when(p.c - k >= 0)
        def _():
            across_stats(p.c - k).start()

    stats[p.c] = mine[...]

    @pl.loop(1, n)
    def _(k):
        @pl.when(p.c + k < n)
        def _():
            arrive(p.c + k).wait_recv()
            arrive_stats(p.c + k).wait_recv()

    key_at = p.c * rows + lax.broadcasted_iota(jnp.int32, (rows, seq), 0)
    query_at = lax.broadcasted_iota(jnp.int32, (rows, seq), 1)
    allowed = key_at <= query_at
    for h in range(heads):
        cols = pl.ds(h * HEAD_DIM, HEAD_DIM)
        queries = kvq_ref[:, :, 2 * width + h * HEAD_DIM:2 * width + (h + 1) * HEAD_DIM].reshape(
            seq, HEAD_DIM
        )
        upstream = g_all[:, :, h * HEAD_DIM:(h + 1) * HEAD_DIM].reshape(seq, HEAD_DIM)
        queries = jnp.where(late, queries, nothing)
        upstream = jnp.where(late, upstream, nothing)
        keys = kvq_ref[p.c, :, pl.ds(h * HEAD_DIM, HEAD_DIM)]
        values = kvq_ref[p.c, :, pl.ds(width + h * HEAD_DIM, HEAD_DIM)]
        delta = jnp.concatenate([stats[s, h:h + 1, :] for s in range(n)], axis=1)
        log_norm = jnp.concatenate([stats[s, heads + h:heads + h + 1, :] for s in range(n)], axis=1)
        scores = contract_last(keys, queries) * scale
        probs = jnp.where(allowed, jnp.exp(jnp.where(allowed, scores - log_norm, 0.0)), 0.0)
        grad_scores = jnp.where(
            allowed, probs * (contract_last(values, upstream) - delta), 0.0
        ).astype(BF16)
        dv_ref[:, cols] = jnp.dot(probs.astype(BF16), upstream, preferred_element_type=F32).astype(BF16)
        dk_ref[:, cols] = (jnp.dot(grad_scores, queries, preferred_element_type=F32) * scale).astype(BF16)

    @pl.loop(1, n)
    def _(k):
        @pl.when(p.c - k >= 0)
        def _():
            across(p.c - k).wait_send()
            across_stats(p.c - k).wait_send()


def params(collective_id, grid=False, vmem=56):
    return pltpu.CompilerParams(
        collective_id=collective_id,
        has_side_effects=True,
        vmem_limit_bytes=vmem * 1024 * 1024,
        **({"dimension_semantics": ("arbitrary",)} if grid else {}),
    )


def plain_route(
    dims, sizes, send_rows, mixed_in, grad_out, dense_gate, dense_up, dense_down,
    expert_gate, expert_up, expert_down, kvq
):
    n, tp, ep = dims
    group = tp * ep
    capacity, pair, chunk = sizes
    rows, width = mixed_in.shape
    part = width // group
    sem = pltpu.SemaphoreType.DMA
    ff = dense_gate.shape[0]
    ff_tile = tile_of(ff, 320)
    weight_spec = pl.BlockSpec((ff_tile, width), lambda i: (i, 0))
    full = pl.BlockSpec((rows, width), lambda i: (0, 0))
    arrived, dense_part = pl.pallas_call(
        functools.partial(dispatch_kernel, dims, ff // ff_tile),
        grid=(ff // ff_tile,),
        out_shape=(
            jax.ShapeDtypeStruct((tp, ep, n, pair, part), BF16),
            jax.ShapeDtypeStruct((rows, width), BF16),
        ),
        in_specs=[ANY, full, full, weight_spec, weight_spec, weight_spec],
        out_specs=(ANY, full),
        scratch_shapes=[pltpu.VMEM((rows, width), F32)]
        + [sem((n,))] * 2 + [sem((ep, n))] * 4 + [sem],
        compiler_params=params(1, True),
        name="dispatch_dense",
    )(send_rows, mixed_in, grad_out, dense_gate, dense_up, dense_down)

    arrived = arrived.reshape(group, n, pair, part)

    def joined(low):
        return arrived[:, :, low:low + capacity].transpose(1, 2, 0, 3).reshape(n * capacity, width)

    head_width = kvq.shape[1] // 3
    eh = expert_gate.shape[1]
    eh_tile = tile_of(eh, 320)
    weight_spec = pl.BlockSpec((1, eh_tile, width), lambda i: (0, i, 0))
    full = pl.BlockSpec((n * capacity, width), lambda i: (0, 0))
    expert_part, kvq_all = pl.pallas_call(
        functools.partial(expert_kernel, dims, eh // eh_tile),
        grid=(eh // eh_tile,),
        out_shape=(
            jax.ShapeDtypeStruct((n * capacity, width), BF16),
            jax.ShapeDtypeStruct((n, rows, 3 * head_width), BF16),
        ),
        in_specs=[full, full, weight_spec, weight_spec, weight_spec, ANY],
        out_specs=(full, ANY),
        scratch_shapes=[pltpu.VMEM((n * capacity, width), F32)] + [sem((n,))] * 2 + [sem],
        compiler_params=params(2, True),
        name="expert_gather",
    )(joined(0), joined(capacity), expert_gate, expert_up, expert_down, kvq)

    dense_chunks = -(-rows // chunk)
    chunks = n + dense_chunks
    expert_part = jnp.pad(
        expert_part.reshape(n, capacity, group, part), ((0, 0), (0, chunk - capacity), (0, 0), (0, 0))
    )
    dense_part = jnp.pad(
        dense_part.reshape(rows, group, part), ((0, dense_chunks * chunk - rows), (0, 0), (0, 0))
    ).reshape(dense_chunks, chunk, group, part)
    parts = jnp.concatenate([expert_part, dense_part], axis=0).transpose(2, 0, 1, 3)
    parts = parts.reshape(tp, ep, chunks, chunk, part)
    returned, dense_sum = pl.pallas_call(
        functools.partial(return_kernel, dims, chunks),
        out_shape=(
            jax.ShapeDtypeStruct((n, chunk, part), BF16),
            jax.ShapeDtypeStruct((dense_chunks, chunk, part), F32),
        ),
        in_specs=[WHOLE],
        out_specs=(WHOLE, WHOLE),
        scratch_shapes=[
            pltpu.VMEM((ep, chunks, chunk, part), BF16),
            pltpu.VMEM((ep, chunks, chunk, part), BF16),
            pltpu.VMEM((ep, chunks, chunk, part), BF16),
            pltpu.VMEM((n, chunk, part), BF16),
        ]
        + [sem((ep, chunks))] * 4 + [sem((n,))] * 2,
        compiler_params=params(3),
        name="return_rows",
    )(parts)
    return returned, dense_sum, kvq_all


def fused_route(
    dims, sizes, send_rows, mixed_in, grad_out, hidden, gain, home_at, out_proj, keys, values, queries,
    dense_gate, dense_up, dense_down, expert_gate, expert_up, expert_down
):
    n, tp, ep = dims
    capacity, pair, chunk = sizes
    rows, width = mixed_in.shape
    part = width // (tp * ep)
    head_width = keys.shape[1]
    heads = head_width // HEAD_DIM
    stat_rows = round_up(heads, 8)
    sem = pltpu.SemaphoreType.DMA
    eh = expert_gate.shape[1]
    dense_chunks = -(-rows // chunk)
    chunks = n + dense_chunks
    blocks = pltpu.VMEM((n, rows, head_width), BF16)
    squares = pltpu.VMEM((heads, rows, n * rows), F32)
    stats = pltpu.VMEM((n, stat_rows, rows), F32)
    own_stats = pltpu.VMEM((stat_rows, rows), F32)
    return pl.pallas_call(
        functools.partial(experts_kernel, dims, capacity),
        out_shape=(
            jax.ShapeDtypeStruct((rows, width), BF16),
            jax.ShapeDtypeStruct((3, rows, head_width), BF16),
        ),
        in_specs=[ANY] + [WHOLE] * 9 + [ANY] * 6,
        out_specs=(WHOLE, WHOLE),
        scratch_shapes=[
            pltpu.VMEM((n, pair, width), BF16),
            pltpu.VMEM((n * capacity, width), BF16),
            pltpu.VMEM((n * capacity, width), BF16),
            pltpu.VMEM((3, max(eh, dense_gate.shape[0]), width), BF16),
            pltpu.VMEM((n * capacity, eh), BF16),
            pltpu.VMEM((n * capacity, eh), BF16),
            pltpu.VMEM((chunks, chunk, width), BF16),
            pltpu.VMEM((ep, chunks, chunk, part), BF16),
            pltpu.VMEM((max(ep - 1, 1), chunks, chunk, part), BF16),
            pltpu.VMEM((max(ep - 1, 1), chunks, chunk, part), BF16),
            pltpu.VMEM((n, chunk, part), BF16),
            pltpu.VMEM((n, chunk, part), BF16),
            pltpu.VMEM((dense_chunks * chunk, part), F32),
            pltpu.VMEM((rows, width), BF16),
            blocks, blocks, blocks, blocks, squares, squares, stats, stats, own_stats, own_stats,
        ]
        + [sem((n,))] * 2 + [sem((ep, n))] * 4 + [sem((ep, chunks))] * 4 + [sem((n,))] * 2
        + [sem((ep,))] * 4 + [sem((6, n))] * 2 + [sem((3,)), sem((1,))],
        compiler_params=params(6, vmem=63),
        name="layer_grads",
    )(
        send_rows, mixed_in, grad_out, hidden, gain.reshape(1, -1), home_at, out_proj,
        keys, values, queries,
        dense_gate, dense_up, dense_down, expert_gate, expert_up, expert_down
    )


def body(
    dims, hidden, grad_out, gain, dense_gate, dense_up, dense_down, expert_gate, expert_up, expert_down,
    out_proj, queries, keys, values, route_ids, route_weights
):
    n, tp, ep = dims
    group = tp * ep
    rows, width = hidden.shape
    part = width // group
    picks = route_ids.shape[1]
    capacity = 5 * rows // (2 * n)
    pair = round_up(2 * capacity, 16)
    chunk = round_up(capacity, 16)
    sem = pltpu.SemaphoreType.DMA
    at = lax.axis_index("tp") * ep + lax.axis_index("ep")

    hidden_f = hidden.astype(F32)
    inverse = lax.rsqrt(jnp.mean(hidden_f * hidden_f, axis=1, keepdims=True) + EPSILON)
    normed = hidden_f * inverse
    mixed_in = (normed * gain).astype(BF16)

    flat_ids = route_ids.reshape(-1)
    hits = (flat_ids[:, None] == lax.iota(jnp.int32, n)[None, :]).astype(BF16)
    order = lax.iota(jnp.int32, picks * rows)
    before = (order[None, :] < order[:, None]).astype(BF16)
    earlier = jnp.dot(before, hits, preferred_element_type=F32)
    slots = jnp.sum(earlier * hits.astype(F32), axis=1).astype(jnp.int32)
    slots = slots.reshape(rows, picks)
    pair_at = (route_ids * pair + slots).T
    home_at = route_ids * chunk + slots
    places = lax.iota(jnp.int32, n * pair)[:, None]
    own_in = lax.dynamic_slice(mixed_in, (0, at * part), (rows, part))
    own_out = lax.dynamic_slice(grad_out, (0, at * part), (rows, part))
    pick_in = sum((places == pair_at[k][None, :]).astype(BF16) for k in range(picks))
    pick_out = [(places == pair_at[k][None, :] + capacity) for k in range(picks)]
    weight_of = sum(
        jnp.sum(jnp.where(pick_out[k], route_weights[:, k][None, :], 0.0), axis=1, keepdims=True)
        for k in range(picks)
    )
    pick_out = sum(hit.astype(BF16) for hit in pick_out)
    send_rows = (
        jnp.dot(pick_in, own_in, preferred_element_type=F32)
        + jnp.dot(pick_out, own_out, preferred_element_type=F32) * weight_of
    ).astype(BF16).reshape(n, pair, part)

    if part % 128 == 0:
        grad_hidden, head_grads = fused_route(
            dims, (capacity, pair, chunk), send_rows, mixed_in, grad_out, hidden, gain, home_at, out_proj,
            keys, values, queries, dense_gate, dense_up, dense_down, expert_gate, expert_up, expert_down
        )
        return (grad_hidden, head_grads[0], head_grads[1], head_grads[2])

    kvq = jnp.concatenate([keys, values, queries], axis=1)
    head_width = queries.shape[1]
    returned, dense_sum, kvq_all = plain_route(
        dims, (capacity, pair, chunk), send_rows, mixed_in, grad_out, dense_gate, dense_up, dense_down,
        expert_gate, expert_up, expert_down, kvq
    )

    home_places = lax.iota(jnp.int32, n * chunk)[None, :]
    take = sum((home_places == home_at[:, k:k + 1]).astype(BF16) for k in range(picks))
    own_total = (
        jnp.dot(take, returned.reshape(n * chunk, part), preferred_element_type=F32)
        + dense_sum.reshape(-1, part)[:rows]
    ).astype(BF16)
    total_grad = pl.pallas_call(
        functools.partial(group_kernel, dims),
        out_shape=jax.ShapeDtypeStruct((tp, ep, rows, part), BF16),
        in_specs=[WHOLE],
        out_specs=WHOLE,
        scratch_shapes=[sem((ep,))] * 4,
        compiler_params=params(4),
        name="group_gather",
    )(own_total)
    total_grad = total_grad.reshape(group, rows, part).transpose(1, 0, 2).reshape(rows, width).astype(F32)
    scaled_grad = total_grad * gain
    grad_hidden = (
        grad_out.astype(F32)
        + inverse * (scaled_grad - normed * jnp.mean(scaled_grad * normed, axis=1, keepdims=True))
    ).astype(BF16)
    grad_heads = contract_last(grad_hidden, out_proj).astype(BF16)

    heads = head_width // HEAD_DIM
    stat_rows = round_up(2 * heads, 8)
    grads = jax.ShapeDtypeStruct((rows, head_width), BF16)
    grad_queries, grad_keys, grad_values = pl.pallas_call(
        functools.partial(attention_kernel, dims),
        out_shape=(grads, grads, grads),
        in_specs=[WHOLE, WHOLE],
        out_specs=(WHOLE, WHOLE, WHOLE),
        scratch_shapes=[
            pltpu.VMEM((n, rows, head_width), BF16),
            pltpu.VMEM((n, stat_rows, rows), F32),
            pltpu.VMEM((stat_rows, rows), F32),
        ]
        + [sem((n,))] * 4,
        compiler_params=params(5),
        name="attention_grads",
    )(grad_heads, kvq_all)
    return (grad_hidden, grad_queries, grad_keys, grad_values)


def solution(mesh):
    dims = (mesh.shape["ctx"], mesh.shape["tp"], mesh.shape["ep"])
    hidden_units = P(("tp", "ep"), None)
    expert_units = P("ctx", ("tp", "ep"), None)
    by_head = P("ctx", ("tp", "ep"))
    return jax.shard_map(
        functools.partial(body, dims),
        mesh=mesh,
        in_specs=(
            P("ctx", None), P("ctx", None), P(),
            hidden_units, hidden_units, hidden_units,
            expert_units, expert_units, expert_units,
            hidden_units, by_head, by_head, by_head,
            P("ctx", None), P("ctx", None),
        ),
        out_specs=(P("ctx", None), by_head, by_head, by_head),
        check_vma=False,
    )
```
